1024 devices in a mesh: dp: 16 (over z, core), fsdp: 64 (over y, x).
Axes of the slice: x: 8, y: 8, z: 8, core: 2. Of those that a mesh axis runs over, the one named last changes fastest.
Arguments:
- qkv: bfloat16 [16, 64, 192, 3, 896], P('dp', 'fsdp'), may hold values from -8 to 8
- grad_out: bfloat16 [16, 64, 192, 896], P('dp', 'fsdp'), may hold values from -6 to 6
- lengths: int32 [16, 64, 3], P(None, 'fsdp'), may hold values from 1 to 128, 192 in all within a row
- moves: int32 [64, 2, 3], P('fsdp'), may hold values from 0 to 15, as said below
- out_weight: bfloat16 [896, 896], P('fsdp'), may hold values from -0.1875 to 0.1875
Outputs:
- home_grad: bfloat16 [16, 64, 192, 3, 896], P('dp', 'fsdp')
- inbox_grad: bfloat16 [16, 64, 128, 3, 896], P('dp', 'fsdp')
- weight_grad: float32 [896, 896], P('fsdp', 'dp')
The draws below stay inside these ranges and needn't reach their ends.
Inputs may be any that keep to these rules, and one draw needn't show every extreme that they name: In each fsdp column the sources of the moves differ from one another, and each destination is (source + 1) mod 16; the clip index is below 3. `lengths`: each device's counts sum to 192.
All inputs are finite; a program needn't handle non-finite values.
Results may differ from the reference program's by a relative error of at most 0.023.
Values may be sent and summed in bfloat16 or wider, within the bound.
No kernel may reach another device: no remote copies, remote signals or barrier semaphores. Data moves between devices by JAX's collectives and lax.ppermute only.
A program may use at most 32 MiB of HBM per device.

```python
import math
import jax
import jax.numpy as jnp
import numpy as np
from jax import lax

HEADS = 8
HSIZE = 112
DOUT = 896
TOK_DEV = 192
CLIP_MAX = 128
MOVES = 2
CLIPS_DEV = 3
HD = 896
N_DP = 16
N_FSDP = 64


def draw_qkv(key, part):
    key = jax.random.fold_in(key, 7)
    shape = (N_DP, N_FSDP, TOK_DEV, 3, HEADS * HSIZE)
    whole = jnp.clip(jax.random.normal(key, shape, jnp.float32), -8.0, 8.0)
    return whole.astype(jnp.bfloat16)


def draw_moves(key, part):
    key = jax.random.fold_in(key, 5)
    keys = jax.random.split(key, N_FSDP)

    def one_column(sub):
        order = jax.random.permutation(sub, N_DP)
        which = jax.random.randint(jax.random.fold_in(sub, 1), (MOVES,), 0, CLIPS_DEV)
        sources = order[:MOVES]
        return jnp.stack([sources, (sources + 1) % N_DP, which], axis=1).astype(jnp.int32)
    return jax.vmap(one_column)(keys)


def block_scale(stream_key, extent, cuts, low, largest):
    factor_of, own = 1.0, jax.random.fold_in(stream_key, 6)
    for dim, shards_of in cuts:
        draws = jnp.exp(jax.random.uniform(jax.random.fold_in(own, dim), (shards_of,), jnp.float32, low / len(cuts), largest / len(cuts)))
        factor_of = factor_of * jnp.repeat(draws, extent[dim] // shards_of).reshape([-1 if axis == dim else 1 for axis in range(len(extent))])
    return factor_of


def profile(count, total, reach, skew):
    portions = [(1 << 20) // math.isqrt(rank ** skew) + 1 for rank in range(2, count + 1)]
    spare, given = total - reach - (count - 1), [1] * (count - 1)
    while spare > 0:
        movable = [i for i in range(count - 1) if given[i] < reach]
        mass, remaining = sum([portions[i] for i in movable]), spare
        for i in movable:
            more = min(reach - given[i], max(1, remaining * portions[i] // mass), spare)
            given[i] = given[i] + more
            spare = spare - more
    return np.array([reach] + given)


def uneven(stream_key, amount, total, most, lean):
    if amount == 2:
        one = jax.random.randint(stream_key, (), max(1, total - most), min(most, total - 1) + 1)
        return jnp.stack([one, total - one])
    sizes = jnp.asarray(profile(amount, total, most, lean), jnp.int32)
    pairs = (amount - 1) // 2
    donor, receiver = sizes[1:1 + 2 * pairs:2], sizes[2:2 + 2 * pairs:2]
    room = jnp.minimum(donor - 1, most - receiver)
    shifted = jax.random.randint(jax.random.fold_in(stream_key, 1), (pairs,), 0, 1 << 20) % (room + 1)
    sizes = sizes.at[1:1 + 2 * pairs:2].set(donor - shifted).at[2:2 + 2 * pairs:2].set(receiver + shifted)
    return sizes[jax.random.permutation(jax.random.fold_in(stream_key, 2), amount)]


def centred(key, shape, scale, reach, cuts=(), kind=jnp.bfloat16):
    result = jax.random.normal(key, shape, jnp.float32) * scale
    if len(cuts) > 0:
        result = block_scale(key, shape, cuts, -0.22, 0.18) * result
    return jnp.clip(result, min=-reach, max=reach).astype(kind)


def setup_inputs(seed: int = 0) -> dict:
    seeds = jax.random.split(jax.random.key(seed), 6)
    return {
        "qkv": draw_qkv(jax.random.fold_in(seeds[5], 71), 0),
        "grad_out": centred(seeds[1], (N_DP, N_FSDP, TOK_DEV, DOUT), 1.0, 6.0, ((0, 16), (1, 64))),
        "lengths": jax.vmap(lambda own: uneven(own, CLIPS_DEV, TOK_DEV, CLIP_MAX, 2))(jax.random.split(seeds[2], N_DP * N_FSDP)).reshape((N_DP, N_FSDP, CLIPS_DEV)).astype(jnp.int32),
        "moves": draw_moves(jax.random.fold_in(seeds[5], 71), 0),
        "out_weight": centred(seeds[4], (HD, DOUT), HD ** -0.5, 0.1875, ((0, 64),)),
    }


def attend(rows, allowed, live):
    length = rows.shape[0]
    split = rows.reshape(length, 3, HEADS, HSIZE).astype(jnp.float32)
    queries = split[:, 0]
    keys = split[:, 1]
    values = split[:, 2]
    scores = jnp.einsum('qhd,khd->hqk', queries, keys) * HSIZE ** (-0.5)
    scores = jnp.where(allowed[None], scores, -1000000000.0)
    probs = jax.nn.softmax(scores, axis=-1).astype(jnp.bfloat16)
    mixed = jnp.einsum('hqk,khd->qhd', probs.astype(jnp.float32), values)
    mixed = jnp.where(live[:, None, None], mixed, 0.0)
    return mixed.reshape(length, HEADS * HSIZE).astype(jnp.bfloat16)

def clip_start(counts, which):
    starts = jnp.cumsum(counts) - counts
    clips = jnp.arange(counts.shape[0], dtype=jnp.int32)
    return (jnp.sum(jnp.where(clips == which, starts, 0)), jnp.sum(jnp.where(clips == which, counts, 0)))

def home_masks(counts, moving, rank):
    ends = jnp.cumsum(counts)
    places = jnp.arange(TOK_DEV, dtype=jnp.int32)
    segment = lax.optimization_barrier(jnp.sum((places[:, None] >= ends[None, :]).astype(jnp.int32), axis=1))
    clips = jnp.arange(counts.shape[0], dtype=jnp.int32)
    gone = jnp.any((moving[:, 0:1] == rank) & (moving[:, 2:3] == clips[None, :]), axis=0)
    stays = jnp.logical_not(jnp.any((segment[:, None] == clips[None, :]) & gone[None, :], axis=1))
    return (segment[:, None] == segment[None, :], stays)

def reference(qkv, grad_out, lengths, moves, out_weight):

    def column(total, index):
        rows = qkv[:, index]
        cotan = grad_out[:, index]
        counts_all = lengths[:, index]
        moving = moves[index]
        padded = jnp.concatenate([rows, jnp.zeros((N_DP, CLIP_MAX, 3, HD), rows.dtype)], axis=1)
        cot_pad = jnp.concatenate([cotan, jnp.zeros((N_DP, CLIP_MAX, DOUT), cotan.dtype)], axis=1)
        box_list = []
        for step in range(MOVES):
            source = moving[step, 0]
            offset, length = clip_start(counts_all[source], moving[step, 2])
            piece_rows = lax.dynamic_slice_in_dim(padded[source], offset.astype(jnp.int32), CLIP_MAX, 0)
            piece_cot = lax.dynamic_slice_in_dim(cot_pad[source], offset.astype(jnp.int32), CLIP_MAX, 0)
            box_list.append((moving[step, 1], piece_rows, piece_cot, length))

        def device(rank, home_rows, home_cot, counts):
            allowed_home, stays = home_masks(counts, moving, rank)
            box_rows = jnp.zeros((CLIP_MAX, 3, HD), jnp.bfloat16)
            box_cot = jnp.zeros((CLIP_MAX, DOUT), jnp.bfloat16)
            box_len = jnp.zeros((), jnp.int32)
            for target, piece_rows, piece_cot, length in box_list:
                mine = target == rank
                box_rows = jnp.where(mine, piece_rows, box_rows)
                box_cot = jnp.where(mine, piece_cot, box_cot)
                box_len = jnp.where(mine, length.astype(jnp.int32), box_len)
            places = jnp.arange(CLIP_MAX, dtype=jnp.int32)
            box_live = places < box_len
            box_allowed = jnp.broadcast_to(box_live[None, :], (CLIP_MAX, CLIP_MAX))

            def forward(home_in, box_in):
                return (attend(home_in, allowed_home, stays), attend(box_in, box_allowed, box_live))
            (mixed_home, mixed_box), pullback = jax.vjp(forward, home_rows, box_rows)
            mixed_all = jnp.concatenate([mixed_home, mixed_box], axis=0)
            cot_all = jnp.concatenate([home_cot, box_cot], axis=0)
            back = lax.dot_general(cot_all, out_weight, (((1,), (1,)), ((), ())), preferred_element_type=jnp.float32).astype(jnp.bfloat16)
            grad_home, grad_box = pullback((back[:TOK_DEV], back[TOK_DEV:]))
            term = lax.dot_general(mixed_all, cot_all, (((0,), (0,)), ((), ())), preferred_element_type=jnp.float32)
            term = lax.optimization_barrier(term.astype(jnp.bfloat16))
            return (grad_home, grad_box, term)
        grad_home, grad_box, terms = jax.vmap(device)(jnp.arange(N_DP, dtype=jnp.int32), rows, cotan, counts_all)
        return (total + lax.optimization_barrier(jnp.sum(terms.astype(jnp.float32), axis=0)), (grad_home, grad_box))
    start = jnp.zeros((HD, DOUT), jnp.float32)
    weight_grad, stacked = lax.scan(column, start, jnp.arange(N_FSDP, dtype=jnp.int32))
    home_grad = jnp.swapaxes(stacked[0], 0, 1)
    inbox_grad = jnp.swapaxes(stacked[1], 0, 1)
    return (home_grad, inbox_grad, weight_grad)
```

```python
import jax
import jax.numpy as jnp
import numpy as np
from jax import lax
from jax.experimental import pallas as pl
from jax.experimental.pallas import tpu as pltpu
from jax.sharding import PartitionSpec as P

HEADS = 8
HSIZE = 112
TOK = 192
CLIP_MAX = 128
FEAT = 896
NZ, NCORE, NY, NX = 8, 2, 8, 8
ROWS = 14
COLS = 56
SCALE = HSIZE ** (-0.5)
TILE = 128
VMEM_BYTES = 48 * 1024 * 1024

Z_GROUPS = [[z * NCORE + c for z in range(NZ)] for c in range(NCORE)]
Y_GROUPS = [[y * NX + x for y in range(NY)] for x in range(NX)]
X_GROUPS = [[y * NX + x for x in range(NX)] for y in range(NY)]
NT = (((1,), (1,)), ((), ()))
NN = (((1,), (0,)), ((), ()))
TN = (((0,), (0,)), ((), ()))


def spread_rows():
    pick = np.zeros((2 * 8 * NY * NX, FEAT), np.float32)
    for b in range(2):
        for f in range(NY * NX):
            for i in range(ROWS // 2):
                pick[b * 512 + 8 * f + i, ROWS * f + 2 * i + b] = 1.0
    return pick.astype(jnp.bfloat16)


def gathered_rows():
    pick = np.zeros((16 * NY * NX, FEAT), np.float32)
    for x in range(NX):
        for y in range(NY):
            for k in range(ROWS):
                pick[(x * NY + y) * 16 + k, ROWS * (y * NX + x) + k] = 1.0
    return pick.astype(jnp.bfloat16)


def dot(a, b, dims):
    return lax.dot_general(a, b, dims, preferred_element_type=jnp.float32)


def window(head):
    low = HSIZE * head
    start = TILE * (low // TILE)
    stop = TILE * (-(-(low + HSIZE) // TILE))
    return start, stop


def own_lanes(head):
    start, stop = window(head)
    lane = lax.broadcasted_iota(jnp.int32, (1, stop - start), 1) + start
    return (lane >= HSIZE * head) & (lane < HSIZE * (head + 1))


def kept(mask, value):
    return jnp.where(mask, value, jnp.zeros((), value.dtype))


def clip_ends(len_ref, rank):
    first = len_ref[0, rank]
    return first, first + len_ref[1, rank]


def forward_body(len_ref, qkv_ref, cot_ref, pick_ref, own_ref, other_ref, prob_ref, mix_ref):
    rank = lax.axis_index("dp")
    first, second = clip_ends(len_ref, rank)

    def segment(shape, dim):
        place = lax.broadcasted_iota(jnp.int32, shape, dim)
        return (place >= first).astype(jnp.int32) + (place >= second).astype(jnp.int32)

    allowed = segment((TOK, TOK), 0) == segment((TOK, TOK), 1)
    tiles = [None] * (FEAT // TILE)
    for head in range(HEADS):
        start, stop = window(head)
        lanes = own_lanes(head)
        query = kept(lanes, qkv_ref[0, :, start:stop])
        value = kept(lanes, qkv_ref[2, :, start:stop])
        scores = dot(query, qkv_ref[1, :, start:stop], NT) * SCALE
        scores = jnp.where(allowed, scores, -1000000000.0)
        peak = jnp.max(scores, axis=1, keepdims=True)
        grown = jnp.exp(scores - peak)
        probs = (grown * (1.0 / jnp.sum(grown, axis=1, keepdims=True))).astype(jnp.bfloat16)
        prob_ref[head] = probs
        part = dot(probs, value, NN)
        for tile in range(start // TILE, stop // TILE):
            piece = part[:, tile * TILE - start:(tile + 1) * TILE - start]
            tiles[tile] = piece if tiles[tile] is None else tiles[tile] + piece
            if HSIZE * (head + 1) >= TILE * (tile + 1):
                mix_ref[:, tile * TILE:(tile + 1) * TILE] = tiles[tile].astype(jnp.bfloat16)

    spread = dot(pick_ref[...], mix_ref[...], NT).astype(jnp.bfloat16)
    half = spread.shape[0] // 2
    core = lax.rem(rank, NCORE)
    cot = cot_ref[...]
    wide = cot.astype(jnp.float32)
    up = pltpu.roll(wide, COLS, 1).astype(jnp.bfloat16)
    down = pltpu.roll(wide, FEAT - COLS, 1).astype(jnp.bfloat16)
    lane = lax.broadcasted_iota(jnp.int32, (1, FEAT), 1)
    low = lax.rem(lane, 2 * COLS) < COLS
    at_zero = jnp.broadcast_to(core, (1, FEAT)) == 0
    zero = jnp.zeros((), jnp.bfloat16)
    straight_low = jnp.where(low, cot, zero)
    straight_high = jnp.where(low, zero, cot)
    moved_low = jnp.where(low, down, zero)
    moved_high = jnp.where(low, zero, up)
    own_ref[...] = (
        dot(spread[:half], jnp.where(at_zero, straight_low, moved_low), NN)
        + dot(spread[half:], jnp.where(at_zero, moved_high, straight_high), NN)
    ).astype(jnp.bfloat16)
    other_ref[...] = (
        dot(spread[:half], jnp.where(at_zero, moved_low, straight_low), NN)
        + dot(spread[half:], jnp.where(at_zero, straight_high, moved_high), NN)
    ).astype(jnp.bfloat16)


def backward_body(
    len_ref, move_ref, qkv_ref, cot_ref, weight_ref, pick_ref, prob_ref,
    home_ref, send_ref, back_ref, full_ref,
):
    rank = lax.axis_index("dp")
    first, second = clip_ends(len_ref, rank)
    begin = jnp.int32(0)
    count = jnp.int32(0)
    for step in range(move_ref.shape[0]):
        mine = move_ref[step, 0] == rank
        clip = move_ref[step, 2]
        clip_begin = jnp.where(clip == 0, 0, jnp.where(clip == 1, first, second))
        clip_end = jnp.where(clip == 0, first, jnp.where(clip == 1, second, TOK))
        begin = jnp.where(mine, clip_begin, begin)
        count = jnp.where(mine, clip_end - clip_begin, count)

    packed = dot(cot_ref[...], weight_ref[...], NT).astype(jnp.bfloat16)
    back_ref[...] = dot(packed, pick_ref[...], NN).astype(jnp.bfloat16)

    place = lax.broadcasted_iota(jnp.int32, (TOK, TILE), 0)
    stays = (place < begin) | (place >= begin + count)
    tiles = [[None] * (FEAT // TILE) for _ in range(3)]
    for head in range(HEADS):
        start, stop = window(head)
        lanes = own_lanes(head)
        query = kept(lanes, qkv_ref[0, :, start:stop])
        key = kept(lanes, qkv_ref[1, :, start:stop])
        back = kept(lanes, back_ref[:, start:stop])
        grad_p = dot(back, qkv_ref[2, :, start:stop], NT)
        probs = prob_ref[head]
        wide = probs.astype(jnp.float32)
        weighted = wide * grad_p
        grad_s = weighted - wide * jnp.sum(weighted, axis=1, keepdims=True)
        grad_s = (grad_s * SCALE).astype(jnp.bfloat16)
        parts = (
            dot(grad_s, key, NN),
            dot(grad_s, query, TN),
            dot(probs, back, TN),
        )
        for which, part in enumerate(parts):
            for tile in range(start // TILE, stop // TILE):
                piece = part[:, tile * TILE - start:(tile + 1) * TILE - start]
                held = tiles[which][tile]
                held = piece if held is None else held + piece
                tiles[which][tile] = held
                if HSIZE * (head + 1) >= TILE * (tile + 1):
                    at = slice(tile * TILE, (tile + 1) * TILE)
                    full_ref[which, :, at] = held.astype(jnp.bfloat16)
                    home_ref[which, :, at] = jnp.where(stays, held, 0.0).astype(jnp.bfloat16)

    row = lax.broadcasted_iota(jnp.int32, (CLIP_MAX, TOK), 0)
    col = lax.broadcasted_iota(jnp.int32, (CLIP_MAX, TOK), 1)
    pick = ((col == row + begin) & (row < count)).astype(jnp.float32).astype(jnp.bfloat16)
    for which in range(3):
        send_ref[which] = dot(pick, full_ref[which], NN).astype(jnp.bfloat16)


def column_body(got_ref, out_ref):
    total = jnp.sum(got_ref[...].astype(jnp.float32), axis=0)
    for z in range(NZ):
        out_ref[z, :, :2 * COLS] = total[:, 2 * COLS * z:2 * COLS * (z + 1)]
        out_ref[z, :, 2 * COLS:] = jnp.zeros((8, TILE - 2 * COLS), jnp.float32)


def in_vmem():
    return pl.BlockSpec(memory_space=pltpu.VMEM)


def in_smem():
    return pl.BlockSpec(memory_space=pltpu.SMEM)


def shape_of(shape, dtype):
    return jax.ShapeDtypeStruct(shape, dtype)


def forward(counts, qkv, cot, pick):
    return pl.pallas_call(
        forward_body,
        out_shape=(
            shape_of((512, FEAT), jnp.bfloat16),
            shape_of((512, FEAT), jnp.bfloat16),
            shape_of((HEADS, TOK, TOK), jnp.bfloat16),
        ),
        in_specs=[in_smem()] + [in_vmem()] * 3,
        out_specs=(in_vmem(),) * 3,
        scratch_shapes=[pltpu.VMEM((TOK, FEAT), jnp.bfloat16)],
        compiler_params=pltpu.CompilerParams(vmem_limit_bytes=VMEM_BYTES),
        cost_estimate=pl.CostEstimate(flops=2_000_000_000, bytes_accessed=8_000_000, transcendentals=300_000),
        name="forward",
    )(counts, qkv, cot, pick)


def backward(counts, moving, qkv, cot, weights, pick, probs):
    return pl.pallas_call(
        backward_body,
        out_shape=(
            shape_of((3, TOK, FEAT), jnp.bfloat16),
            shape_of((3, CLIP_MAX, FEAT), jnp.bfloat16),
        ),
        in_specs=[in_smem()] * 2 + [in_vmem()] * 5,
        out_specs=(in_vmem(),) * 2,
        scratch_shapes=[
            pltpu.VMEM((TOK, FEAT), jnp.bfloat16),
            pltpu.VMEM((3, TOK, FEAT), jnp.bfloat16),
        ],
        compiler_params=pltpu.CompilerParams(vmem_limit_bytes=VMEM_BYTES),
        cost_estimate=pl.CostEstimate(flops=2_000_000_000, bytes_accessed=8_000_000, transcendentals=0),
        name="backward",
    )(counts, moving, qkv, cot, weights, pick, probs)


def column_sum(got):
    return pl.pallas_call(
        column_body,
        out_shape=shape_of((NZ, 8, TILE), jnp.float32),
        in_specs=[in_vmem()],
        out_specs=in_vmem(),
        name="column_sum",
    )(got)


def local(qkv, grad_out, lengths, moves, out_weight):
    rows = jnp.transpose(qkv[0, 0], (1, 0, 2))
    cot = grad_out[0, 0]
    counts = jnp.transpose(lengths[:, 0])
    moving = moves[0]
    spread = jnp.asarray(spread_rows())
    gathered = jnp.asarray(gathered_rows())

    with jax.named_scope("weights_y"):
        shard = jnp.pad(out_weight, ((0, 16 - ROWS), (0, 0)))
        copies = jnp.broadcast_to(shard[None], (NY,) + shard.shape)
        column = lax.all_to_all(copies, "fsdp", 0, 0, tiled=True, axis_index_groups=Y_GROUPS)
    column, rows, cot = lax.optimization_barrier((column, rows, cot))
    with jax.named_scope("weights_x"):
        weights = lax.all_gather(
            column.reshape(NY * 16, FEAT), "fsdp", axis=0, tiled=True, axis_index_groups=X_GROUPS
        )

    own, other, probs = forward(counts, rows, cot, spread)
    swapped = lax.ppermute(
        other, "dp", [(z * NCORE + c, z * NCORE + 1 - c) for z in range(NZ) for c in range(NCORE)]
    )
    pair = (own.astype(jnp.float32) + swapped.astype(jnp.float32)).astype(jnp.bfloat16)
    with jax.named_scope("reduce_fsdp"):
        got = lax.all_to_all(pair.reshape(NY * NX, 8, FEAT), "fsdp", 0, 0, tiled=True)
    weights, got = lax.optimization_barrier((weights, got))

    home, send = backward(counts, moving, rows, cot, weights, gathered, probs)
    got, send = lax.optimization_barrier((got, send))
    inbox = lax.ppermute(send, "dp", [(i, (i + 1) % (NZ * NCORE)) for i in range(NZ * NCORE)])

    with jax.named_scope("reduce_z"):
        parts = lax.all_to_all(column_sum(got), "dp", 0, 0, tiled=True, axis_index_groups=Z_GROUPS)
    total = jnp.sum(parts, axis=0)[:ROWS // 2, :2 * COLS]
    weight_grad = total.reshape(ROWS, COLS)
    return (
        jnp.transpose(home, (1, 0, 2))[None, None],
        jnp.transpose(inbox, (1, 0, 2))[None, None],
        weight_grad,
    )


def solution(mesh):
    placed = (
        P("dp", "fsdp", None, None, None),
        P("dp", "fsdp", None, None),
        P(None, "fsdp", None),
        P("fsdp", None, None),
        P("fsdp", None),
    )
    return jax.shard_map(
        local,
        mesh=mesh,
        in_specs=placed,
        out_specs=(
            P("dp", "fsdp", None, None, None),
            P("dp", "fsdp", None, None, None),
            P("fsdp", "dp"),
        ),
        check_vma=False,
    )
```

```python
import jax
import jax.numpy as jnp
import numpy as np
from jax import lax
from jax.experimental import pallas as pl
from jax.experimental.pallas import tpu as pltpu
from jax.sharding import PartitionSpec as P

HEADS = 8
HSIZE = 112
TOK = 192
CLIP_MAX = 128
FEAT = 896
NZ, NCORE, NY, NX = 8, 2, 8, 8
ROWS = 14
COLS = 56
SCALE = HSIZE ** (-0.5)
TILE = 128
VMEM_BYTES = 48 * 1024 * 1024

Y_GROUPS = [[y * NX + x for y in range(NY)] for x in range(NX)]
X_GROUPS = [[y * NX + x for x in range(NX)] for y in range(NY)]
PLANE_GROUPS = [
    [(z * NCORE + c) * NY * NX + y * NX + x for z in range(NZ) for y in range(NY)]
    for c in range(NCORE)
    for x in range(NX)
]
NT = (((1,), (1,)), ((), ()))
NN = (((1,), (0,)), ((), ()))
TN = (((0,), (0,)), ((), ()))


def dot(a, b, dims):
    return lax.dot_general(a, b, dims, preferred_element_type=jnp.float32)


def window(head):
    low = HSIZE * head
    start = TILE * (low // TILE)
    stop = TILE * (-(-(low + HSIZE) // TILE))
    return start, stop


def own_lanes(head):
    start, stop = window(head)
    lane = lax.broadcasted_iota(jnp.int32, (1, stop - start), 1) + start
    return (lane >= HSIZE * head) & (lane < HSIZE * (head + 1))


def gathered_lanes(width):
    row = lax.broadcasted_iota(jnp.int32, (TILE, width), 0)
    lane = lax.broadcasted_iota(jnp.int32, (TILE, width), 1)
    inner = row & 15
    return jnp.where(inner < ROWS, lane - (row >> 4) * ROWS - inner, -1)


def kept(mask, value):
    return jnp.where(mask, value, jnp.zeros((), value.dtype))


def as_bf16(mask):
    return mask.astype(jnp.float32).astype(jnp.bfloat16)


def clip_ends(len_ref, rank):
    first = len_ref[0, rank]
    return first, first + len_ref[1, rank]


def forward_body(len_ref, qkv_ref, cot_ref, own_ref, other_ref, prob_ref, mix_ref, term_ref):
    rank = lax.axis_index("dp")
    first, second = clip_ends(len_ref, rank)

    def segment(shape, dim):
        place = lax.broadcasted_iota(jnp.int32, shape, dim)
        return (place >= first).astype(jnp.int32) + (place >= second).astype(jnp.int32)

    allowed = segment((TOK, TOK), 0) == segment((TOK, TOK), 1)
    for head in range(HEADS):
        start, stop = window(head)
        lanes = own_lanes(head)
        query = kept(lanes, qkv_ref[0, :, start:stop])
        value = kept(lanes, qkv_ref[2, :, start:stop])
        scores = dot(query, qkv_ref[1, :, start:stop], NT) * SCALE
        scores = jnp.where(allowed, scores, -1000000000.0)
        peak = jnp.max(scores, axis=1, keepdims=True)
        grown = jnp.exp(scores - peak)
        probs = (grown * (1.0 / jnp.sum(grown, axis=1, keepdims=True))).astype(jnp.bfloat16)
        prob_ref[head] = probs
        mixed = dot(probs, value, NN)
        offset = HSIZE * head - start
        if offset:
            mixed = pltpu.roll(mixed, stop - start - offset, 1)
        mix_ref[:, head * TILE:(head + 1) * TILE] = mixed[:, :TILE].astype(jnp.bfloat16)

    term_ref[...] = dot(cot_ref[...], mix_ref[...], TN)
    core = lax.rem(rank, NCORE)
    for z in range(NZ):
        for ref, part in ((own_ref, core), (other_ref, 1 - core)):
            rows = pl.ds(pl.multiple_of(2 * COLS * z + COLS * part, 8), COLS)
            for y in range(NY):
                ref[z * NY + y] = term_ref[rows, y * TILE:(y + 1) * TILE].astype(jnp.bfloat16)


def backward_body(
    len_ref, move_ref, qkv_ref, cot_ref, weight_ref, prob_ref,
    home_ref, send_ref, full_ref,
):
    rank = lax.axis_index("dp")
    first, second = clip_ends(len_ref, rank)
    begin = jnp.int32(0)
    count = jnp.int32(0)
    for step in range(move_ref.shape[0]):
        mine = move_ref[step, 0] == rank
        clip = move_ref[step, 2]
        clip_begin = jnp.where(clip == 0, 0, jnp.where(clip == 1, first, second))
        clip_end = jnp.where(clip == 0, first, jnp.where(clip == 1, second, TOK))
        begin = jnp.where(mine, clip_begin, begin)
        count = jnp.where(mine, clip_end - clip_begin, count)

    place = lax.broadcasted_iota(jnp.int32, (TOK, TILE), 0)
    stays = (place < begin) | (place >= begin + count)
    cot = cot_ref[...]
    tiles = [[None] * (FEAT // TILE) for _ in range(3)]
    for head in range(HEADS):
        start, stop = window(head)
        lanes = own_lanes(head)
        query = kept(lanes, qkv_ref[0, :, start:stop])
        key = kept(lanes, qkv_ref[1, :, start:stop])
        weights = weight_ref[:, head].reshape(TILE, FEAT)
        packed = dot(cot, weights, NT).astype(jnp.bfloat16)
        offset = HSIZE * head - start
        pick = as_bf16(gathered_lanes(stop - start) == offset)
        back = dot(packed, pick, NN).astype(jnp.bfloat16)
        grad_p = dot(back, qkv_ref[2, :, start:stop], NT)
        probs = prob_ref[head]
        wide = probs.astype(jnp.float32)
        weighted = wide * grad_p
        grad_s = weighted - wide * jnp.sum(weighted, axis=1, keepdims=True)
        grad_s = (grad_s * SCALE).astype(jnp.bfloat16)
        parts = (
            dot(grad_s, key, NN),
            dot(grad_s, query, TN),
            dot(probs, back, TN),
        )
        for which, part in enumerate(parts):
            for tile in range(start // TILE, stop // TILE):
                piece = part[:, tile * TILE - start:(tile + 1) * TILE - start]
                held = tiles[which][tile]
                held = piece if held is None else held + piece
                tiles[which][tile] = held
                if HSIZE * (head + 1) >= TILE * (tile + 1):
                    at = slice(tile * TILE, (tile + 1) * TILE)
                    full_ref[which, :, at] = held.astype(jnp.bfloat16)
                    home_ref[which, :, at] = jnp.where(stays, held, 0.0).astype(jnp.bfloat16)

    row = lax.broadcasted_iota(jnp.int32, (CLIP_MAX, TOK), 0)
    col = lax.broadcasted_iota(jnp.int32, (CLIP_MAX, TOK), 1)
    pick = as_bf16((col == row + begin) & (row < count))
    for which in range(3):
        send_ref[which] = dot(pick, full_ref[which], NN).astype(jnp.bfloat16)


def plane_body(got_ref, out_ref, turned_ref):
    total = jnp.sum(got_ref[...].astype(jnp.float32), axis=0)
    total = jnp.concatenate([total, jnp.zeros((TILE - COLS, TILE), jnp.float32)], axis=0)
    turned_ref[...] = jnp.transpose(total)
    out_ref[...] = jnp.zeros(out_ref.shape, jnp.float32)
    for x in range(NX):
        for b in range(2):
            rows = turned_ref[pl.ds(ROWS * x + b, ROWS // 2, stride=2), :]
            out_ref[x, :ROWS // 2, b * COLS:(b + 1) * COLS] = rows[:, :COLS]


def row_body(got_ref, out_ref):
    total = jnp.sum(got_ref[...], axis=0)
    for b in range(2):
        out_ref[pl.ds(b, ROWS // 2, stride=2), :] = total[:ROWS // 2, b * COLS:(b + 1) * COLS]


def in_vmem():
    return pl.BlockSpec(memory_space=pltpu.VMEM)


def in_smem():
    return pl.BlockSpec(memory_space=pltpu.SMEM)


def shape_of(shape, dtype):
    return jax.ShapeDtypeStruct(shape, dtype)


def forward(counts, qkv, cot):
    return pl.pallas_call(
        forward_body,
        out_shape=(
            shape_of((NZ * NY, COLS, TILE), jnp.bfloat16),
            shape_of((NZ * NY, COLS, TILE), jnp.bfloat16),
            shape_of((HEADS, TOK, TOK), jnp.bfloat16),
        ),
        in_specs=[in_smem()] + [in_vmem()] * 2,
        out_specs=(in_vmem(),) * 3,
        scratch_shapes=[
            pltpu.VMEM((TOK, HEADS * TILE), jnp.bfloat16),
            pltpu.VMEM((FEAT, HEADS * TILE), jnp.float32),
        ],
        compiler_params=pltpu.CompilerParams(vmem_limit_bytes=VMEM_BYTES),
        cost_estimate=pl.CostEstimate(flops=2_000_000_000, bytes_accessed=8_000_000, transcendentals=300_000),
        name="forward",
    )(counts, qkv, cot)


def backward(counts, moving, qkv, cot, weights, probs):
    return pl.pallas_call(
        backward_body,
        out_shape=(
            shape_of((3, TOK, FEAT), jnp.bfloat16),
            shape_of((3, CLIP_MAX, FEAT), jnp.bfloat16),
        ),
        in_specs=[in_smem()] * 2 + [in_vmem()] * 4,
        out_specs=(in_vmem(),) * 2,
        scratch_shapes=[pltpu.VMEM((3, TOK, FEAT), jnp.bfloat16)],
        compiler_params=pltpu.CompilerParams(vmem_limit_bytes=VMEM_BYTES),
        cost_estimate=pl.CostEstimate(flops=2_000_000_000, bytes_accessed=8_000_000, transcendentals=0),
        name="backward",
    )(counts, moving, qkv, cot, weights, probs)


def plane_sum(got):
    return pl.pallas_call(
        plane_body,
        out_shape=shape_of((NX, 8, TILE), jnp.float32),
        in_specs=[in_vmem()],
        out_specs=in_vmem(),
        scratch_shapes=[pltpu.VMEM((TILE, TILE), jnp.float32)],
        name="plane_sum",
    )(got)


def row_sum(got):
    return pl.pallas_call(
        row_body,
        out_shape=shape_of((ROWS, COLS), jnp.float32),
        in_specs=[in_vmem()],
        out_specs=in_vmem(),
        name="row_sum",
    )(got)


def local(qkv, grad_out, lengths, moves, out_weight):
    rows = jnp.transpose(qkv[0, 0], (1, 0, 2))
    cot = grad_out[0, 0]
    counts = jnp.transpose(lengths[:, 0])
    moving = moves[0]

    with jax.named_scope("weights_y"):
        shard = jnp.pad(out_weight, ((0, 16 - ROWS), (0, 0)))
        copies = jnp.broadcast_to(shard[None], (NY,) + shard.shape)
        column = lax.all_to_all(copies, "fsdp", 0, 0, tiled=True, axis_index_groups=Y_GROUPS)
    column, counts = lax.optimization_barrier((column, counts))
    with jax.named_scope("weights_x"):
        weights = lax.all_gather(
            column.reshape(NY * 16, FEAT), "fsdp", axis=0, tiled=True, axis_index_groups=X_GROUPS
        )

    own, other, probs = forward(counts, rows, cot)
    swapped = lax.ppermute(
        other, "dp", [(z * NCORE + c, z * NCORE + 1 - c) for z in range(NZ) for c in range(NCORE)]
    )
    pair = (own.astype(jnp.float32) + swapped.astype(jnp.float32)).astype(jnp.bfloat16)
    with jax.named_scope("reduce_zy"):
        got = lax.all_to_all(
            pair, ("dp", "fsdp"), 0, 0, tiled=True, axis_index_groups=PLANE_GROUPS
        )
    weights, got = lax.optimization_barrier((weights, got))

    home, send = backward(
        counts, moving, rows, cot, weights.reshape(NX, NY, 16, FEAT), probs
    )
    got, send = lax.optimization_barrier((got, send))
    inbox = lax.ppermute(send, "dp", [(i, (i + 1) % (NZ * NCORE)) for i in range(NZ * NCORE)])

    with jax.named_scope("reduce_x"):
        parts = lax.all_to_all(plane_sum(got), "fsdp", 0, 0, tiled=True, axis_index_groups=X_GROUPS)
    return (
        jnp.transpose(home, (1, 0, 2))[None, None],
        jnp.transpose(inbox, (1, 0, 2))[None, None],
        row_sum(parts),
    )


def solution(mesh):
    placed = (
        P("dp", "fsdp", None, None, None),
        P("dp", "fsdp", None, None),
        P(None, "fsdp", None),
        P("fsdp", None, None),
        P("fsdp", None),
    )
    return jax.shard_map(
        local,
        mesh=mesh,
        in_specs=placed,
        out_specs=(
            P("dp", "fsdp", None, None, None),
            P("dp", "fsdp", None, None, None),
            P("fsdp", "dp"),
        ),
        check_vma=False,
    )
```

```python
import jax
import jax.numpy as jnp
import numpy as np
from jax import lax
from jax.experimental import pallas as pl
from jax.experimental.pallas import tpu as pltpu
from jax.sharding import PartitionSpec as P

HEADS = 8
HSIZE = 112
TOK = 192
CLIP_MAX = 128
FEAT = 896
NZ, NCORE, NY, NX = 8, 2, 8, 8
ROWS = 14
COLS = 56
SCALE = HSIZE ** (-0.5)
TILE = 128
VMEM_BYTES = 14 * 1024 * 1024

Y_GROUPS = [[y * NX + x for y in range(NY)] for x in range(NX)]
X_GROUPS = [[y * NX + x for x in range(NX)] for y in range(NY)]
PLANE_GROUPS = [
    [(z * NCORE + c) * NY * NX + y * NX + x for z in range(NZ) for y in range(NY)]
    for c in range(NCORE)
    for x in range(NX)
]
NT = (((1,), (1,)), ((), ()))
NN = (((1,), (0,)), ((), ()))
TN = (((0,), (0,)), ((), ()))


def dot(a, b, dims):
    return lax.dot_general(a, b, dims, preferred_element_type=jnp.float32)


def window(head):
    low = HSIZE * head
    start = TILE * (low // TILE)
    stop = TILE * (-(-(low + HSIZE) // TILE))
    return start, stop


def own_lanes(head):
    start, stop = window(head)
    lane = lax.broadcasted_iota(jnp.int32, (1, stop - start), 1) + start
    return (lane >= HSIZE * head) & (lane < HSIZE * (head + 1))


def gathered_lanes(width):
    row = lax.broadcasted_iota(jnp.int32, (TILE, width), 0)
    lane = lax.broadcasted_iota(jnp.int32, (TILE, width), 1)
    inner = row & 15
    return jnp.where(inner < ROWS, lane - (row >> 4) * ROWS - inner, -1)


def kept(mask, value):
    return jnp.where(mask, value, jnp.zeros((), value.dtype))


def as_bf16(mask):
    return mask.astype(jnp.float32).astype(jnp.bfloat16)


def clip_ends(len_ref, rank):
    first = len_ref[0, 0, rank]
    return first, first + len_ref[1, 0, rank]


def moved_clip(len_ref, move_ref, source):
    first, second = clip_ends(len_ref, source)
    begin = jnp.int32(0)
    count = jnp.int32(0)
    for step in range(move_ref.shape[0]):
        mine = move_ref[step, 0] == source
        clip = move_ref[step, 2]
        clip_begin = jnp.where(clip == 0, 0, jnp.where(clip == 1, first, second))
        clip_end = jnp.where(clip == 0, first, jnp.where(clip == 1, second, TOK))
        begin = jnp.where(mine, clip_begin, begin)
        count = jnp.where(mine, clip_end - clip_begin, count)
    return begin, count


def attention(query, key, allowed):
    scores = dot(query, key, NT) * SCALE
    scores = jnp.where(allowed, scores, -1000000000.0)
    peak = jnp.max(scores, axis=1, keepdims=True)
    grown = jnp.exp(scores - peak)
    return grown * (1.0 / jnp.sum(grown, axis=1, keepdims=True))


def pack_body(len_ref, move_ref, qkv_ref, cot_ref, box_ref):
    rank = lax.axis_index("dp")
    begin, count = moved_clip(len_ref, move_ref, rank)
    row = lax.broadcasted_iota(jnp.int32, (CLIP_MAX, TOK), 0)
    col = lax.broadcasted_iota(jnp.int32, (CLIP_MAX, TOK), 1)
    pick = as_bf16((col == row + begin) & (row < count))
    for which in range(3):
        box_ref[which] = dot(pick, qkv_ref[which], NN).astype(jnp.bfloat16)
    box_ref[3] = dot(pick, cot_ref[...], NN).astype(jnp.bfloat16)


def box_body(len_ref, move_ref, box_ref, prob_ref):
    rank = lax.axis_index("dp")
    _, count = moved_clip(len_ref, move_ref, lax.rem(rank + NZ * NCORE - 1, NZ * NCORE))
    row = lax.broadcasted_iota(jnp.int32, (CLIP_MAX, CLIP_MAX), 0)
    col = lax.broadcasted_iota(jnp.int32, (CLIP_MAX, CLIP_MAX), 1)
    for head in range(HEADS):
        start, stop = window(head)
        query = kept(own_lanes(head), box_ref[0, :, start:stop])
        probs = attention(query, box_ref[1, :, start:stop], col < count)
        prob_ref[head] = jnp.where(row < count, probs, 0.0).astype(jnp.bfloat16)


def forward_body(len_ref, qkv_ref, cot_ref, own_ref, other_ref, prob_ref, mix_ref, term_ref):
    rank = lax.axis_index("dp")
    first, second = clip_ends(len_ref, rank)

    def segment(shape, dim):
        place = lax.broadcasted_iota(jnp.int32, shape, dim)
        return (place >= first).astype(jnp.int32) + (place >= second).astype(jnp.int32)

    allowed = segment((TOK, TOK), 0) == segment((TOK, TOK), 1)
    for head in range(HEADS):
        start, stop = window(head)
        lanes = own_lanes(head)
        query = kept(lanes, qkv_ref[0, :, start:stop])
        value = kept(lanes, qkv_ref[2, :, start:stop])
        probs = attention(query, qkv_ref[1, :, start:stop], allowed).astype(jnp.bfloat16)
        prob_ref[head] = probs
        mixed = dot(probs, value, NN)
        offset = HSIZE * head - start
        if offset:
            mixed = pltpu.roll(mixed, stop - start - offset, 1)
        mix_ref[:, head * TILE:(head + 1) * TILE] = mixed[:, :TILE].astype(jnp.bfloat16)

    term_ref[...] = dot(cot_ref[...], mix_ref[...], TN)
    core = lax.rem(rank, NCORE)
    for z in range(NZ):
        for ref, part in ((own_ref, core), (other_ref, 1 - core)):
            rows = pl.ds(pl.multiple_of(2 * COLS * z + COLS * part, 8), COLS)
            for y in range(NY):
                ref[z * NY + y] = term_ref[rows, y * TILE:(y + 1) * TILE].astype(jnp.bfloat16)


class Tiles:
    def __init__(self, ref, mask):
        self.ref = ref
        self.mask = mask
        self.held = [[None] * (FEAT // TILE) for _ in range(3)]

    def add(self, which, head, part):
        start, stop = window(head)
        for tile in range(start // TILE, stop // TILE):
            piece = part[:, tile * TILE - start:(tile + 1) * TILE - start]
            held = self.held[which][tile]
            held = piece if held is None else held + piece
            self.held[which][tile] = held
            if HSIZE * (head + 1) >= TILE * (tile + 1):
                if self.mask is not None:
                    held = jnp.where(self.mask, held, 0.0)
                self.ref[which, :, tile * TILE:(tile + 1) * TILE] = held.astype(jnp.bfloat16)


def add_gradient(tiles, head, rows_ref, probs, back):
    start, stop = window(head)
    lanes = own_lanes(head)
    query = kept(lanes, rows_ref[0, :, start:stop])
    key = kept(lanes, rows_ref[1, :, start:stop])
    grad_p = dot(back, rows_ref[2, :, start:stop], NT)
    wide = probs.astype(jnp.float32)
    weighted = wide * grad_p
    grad_s = weighted - wide * jnp.sum(weighted, axis=1, keepdims=True)
    grad_s = (grad_s * SCALE).astype(jnp.bfloat16)
    tiles.add(0, head, dot(grad_s, key, NN))
    tiles.add(1, head, dot(grad_s, query, TN))
    tiles.add(2, head, dot(probs, back, TN))


def backward_body(
    len_ref, move_ref, qkv_ref, cot_ref, box_ref, prob_ref, box_prob_ref, weight_ref,
    home_ref, inbox_ref, held_ref, both_ref, sem,
):
    def weight_copy(head):
        return pltpu.make_async_copy(weight_ref.at[:, head], held_ref.at[head], sem.at[head])

    for head in range(HEADS):
        weight_copy(head).start()
    rank = lax.axis_index("dp")
    begin, count = moved_clip(len_ref, move_ref, rank)
    place = lax.broadcasted_iota(jnp.int32, (TOK, TILE), 0)
    home = Tiles(home_ref, (place < begin) | (place >= begin + count))
    inbox = Tiles(inbox_ref, None)
    both_ref[:TOK] = cot_ref[...]
    both_ref[TOK:] = box_ref[3]
    for head in range(HEADS):
        start, stop = window(head)
        weight_copy(head).wait()
        weights = held_ref[head].reshape(TILE, FEAT)
        packed = dot(both_ref[...], weights, NT).astype(jnp.bfloat16)
        pick = as_bf16(gathered_lanes(stop - start) == HSIZE * head - start)
        back = dot(packed, pick, NN).astype(jnp.bfloat16)
        add_gradient(home, head, qkv_ref, prob_ref[head], back[:TOK])
        add_gradient(inbox, head, box_ref, box_prob_ref[head], back[TOK:])


def plane_body(got_ref, out_ref, turned_ref):
    total = jnp.sum(got_ref[...].astype(jnp.float32), axis=0)
    total = jnp.concatenate([total, jnp.zeros((TILE - COLS, TILE), jnp.float32)], axis=0)
    turned_ref[...] = jnp.transpose(total)
    out_ref[...] = jnp.zeros(out_ref.shape, jnp.float32)
    for x in range(NX):
        for b in range(2):
            rows = turned_ref[pl.ds(ROWS * x + b, ROWS // 2, stride=2), :]
            out_ref[x, :ROWS // 2, b * COLS:(b + 1) * COLS] = rows[:, :COLS]


def row_body(got_ref, out_ref):
    total = jnp.sum(got_ref[...], axis=0)
    for b in range(2):
        out_ref[pl.ds(b, ROWS // 2, stride=2), :] = total[:ROWS // 2, b * COLS:(b + 1) * COLS]


def in_vmem():
    return pl.BlockSpec(memory_space=pltpu.VMEM)


def in_smem():
    return pl.BlockSpec(memory_space=pltpu.SMEM)


def shape_of(shape, dtype):
    return jax.ShapeDtypeStruct(shape, dtype)


def forward(counts, qkv, cot):
    return pl.pallas_call(
        forward_body,
        out_shape=(
            shape_of((NZ * NY, COLS, TILE), jnp.bfloat16),
            shape_of((NZ * NY, COLS, TILE), jnp.bfloat16),
            shape_of((HEADS, TOK, TOK), jnp.bfloat16),
        ),
        in_specs=[in_smem()] + [in_vmem()] * 2,
        out_specs=(in_vmem(),) * 3,
        scratch_shapes=[
            pltpu.VMEM((TOK, HEADS * TILE), jnp.bfloat16),
            pltpu.VMEM((FEAT, HEADS * TILE), jnp.float32),
        ],
        compiler_params=pltpu.CompilerParams(vmem_limit_bytes=VMEM_BYTES),
        cost_estimate=pl.CostEstimate(flops=2_000_000_000, bytes_accessed=8_000_000, transcendentals=300_000),
        name="forward",
    )(counts, qkv, cot)


def pack(counts, moving, qkv, cot):
    return pl.pallas_call(
        pack_body,
        out_shape=shape_of((4, CLIP_MAX, FEAT), jnp.bfloat16),
        in_specs=[in_smem()] * 2 + [in_vmem()] * 2,
        out_specs=in_vmem(),
        compiler_params=pltpu.CompilerParams(vmem_limit_bytes=VMEM_BYTES),
        cost_estimate=pl.CostEstimate(flops=500_000_000, bytes_accessed=2_000_000, transcendentals=0),
        name="pack",
    )(counts, moving, qkv, cot)


def box_forward(counts, moving, box):
    return pl.pallas_call(
        box_body,
        out_shape=shape_of((HEADS, CLIP_MAX, CLIP_MAX), jnp.bfloat16),
        in_specs=[in_smem()] * 2 + [in_vmem()],
        out_specs=in_vmem(),
        compiler_params=pltpu.CompilerParams(vmem_limit_bytes=VMEM_BYTES),
        cost_estimate=pl.CostEstimate(flops=1_000_000_000, bytes_accessed=2_000_000, transcendentals=100_000),
        name="box_forward",
    )(counts, moving, box)


def backward(counts, moving, qkv, cot, box, probs, box_probs, weights):
    return pl.pallas_call(
        backward_body,
        out_shape=(
            shape_of((3, TOK, FEAT), jnp.bfloat16),
            shape_of((3, CLIP_MAX, FEAT), jnp.bfloat16),
        ),
        in_specs=[in_smem()] * 2 + [in_vmem()] * 5 + [pl.BlockSpec(memory_space=pl.ANY)],
        out_specs=(in_vmem(),) * 2,
        scratch_shapes=[
            pltpu.VMEM((HEADS, NX, 16, FEAT), jnp.bfloat16),
            pltpu.VMEM((TOK + CLIP_MAX, FEAT), jnp.bfloat16),
            pltpu.SemaphoreType.DMA((HEADS,)),
        ],
        compiler_params=pltpu.CompilerParams(vmem_limit_bytes=VMEM_BYTES),
        cost_estimate=pl.CostEstimate(flops=8_000_000_000, bytes_accessed=8_000_000, transcendentals=0),
        name="backward",
    )(counts, moving, qkv, cot, box, probs, box_probs, weights)


def plane_sum(got):
    return pl.pallas_call(
        plane_body,
        out_shape=shape_of((NX, 8, TILE), jnp.float32),
        in_specs=[in_vmem()],
        out_specs=in_vmem(),
        scratch_shapes=[pltpu.VMEM((TILE, TILE), jnp.float32)],
        compiler_params=pltpu.CompilerParams(vmem_limit_bytes=VMEM_BYTES),
        name="plane_sum",
    )(got)


def row_sum(got):
    return pl.pallas_call(
        row_body,
        out_shape=shape_of((ROWS, COLS), jnp.float32),
        in_specs=[in_vmem()],
        out_specs=in_vmem(),
        compiler_params=pltpu.CompilerParams(vmem_limit_bytes=VMEM_BYTES),
        name="row_sum",
    )(got)


def local(qkv, grad_out, lengths, moves, out_weight):
    rows = jnp.transpose(qkv[0, 0], (1, 0, 2))
    cot = grad_out[0, 0]
    counts = jnp.transpose(lengths, (2, 1, 0))
    moving = moves[0]
    ranks = NZ * NCORE

    with jax.named_scope("weights_y"):
        copies = jnp.pad(
            jnp.broadcast_to(out_weight[None], (NY,) + out_weight.shape),
            ((0, 0), (0, 16 - ROWS), (0, 0)),
        )
        column = lax.all_to_all(copies, "fsdp", 0, 0, tiled=True, axis_index_groups=Y_GROUPS)

    send = pack(counts, moving, rows, cot)
    send, later = lax.optimization_barrier((send, counts))
    box = lax.ppermute(send, "dp", [(i, (i + 1) % ranks) for i in range(ranks)])
    own, other, probs = forward(later, rows, cot)
    column, other = lax.optimization_barrier((column, other))
    with jax.named_scope("weights_x"):
        weights = lax.all_gather(
            column.reshape(NY * 16, FEAT), "fsdp", axis=0, tiled=True, axis_index_groups=X_GROUPS
        )
    swapped = lax.ppermute(other, "dp", [(i, i + 1 - 2 * (i % NCORE)) for i in range(ranks)])
    pair = (own.astype(jnp.float32) + swapped.astype(jnp.float32)).astype(jnp.bfloat16)
    with jax.named_scope("reduce_zy"):
        got = lax.all_to_all(
            pair, ("dp", "fsdp"), 0, 0, tiled=True, axis_index_groups=PLANE_GROUPS
        )
    box_probs = box_forward(counts, moving, box)
    plane = plane_sum(got)
    weights, _ = lax.optimization_barrier((weights, plane))
    with jax.named_scope("reduce_x"):
        parts = lax.all_to_all(plane, "fsdp", 0, 0, tiled=True, axis_index_groups=X_GROUPS)
    home, inbox = backward(
        counts, moving, rows, cot, box, probs, box_probs, weights.reshape(NX, NY, 16, FEAT)
    )
    return (
        jnp.transpose(home, (1, 0, 2))[None, None],
        jnp.transpose(inbox, (1, 0, 2))[None, None],
        row_sum(parts),
    )


def solution(mesh):
    placed = (
        P("dp", "fsdp", None, None, None),
        P("dp", "fsdp", None, None),
        P(None, "fsdp", None),
        P("fsdp", None, None),
        P("fsdp", None),
    )
    return jax.shard_map(
        local,
        mesh=mesh,
        in_specs=placed,
        out_specs=(
            P("dp", "fsdp", None, None, None),
            P("dp", "fsdp", None, None, None),
            P("fsdp", "dp"),
        ),
        check_vma=False,
    )
```

```python
import jax
import jax.numpy as jnp
import numpy as np
from jax import lax
from jax.experimental import pallas as pl
from jax.experimental.pallas import tpu as pltpu
from jax.sharding import PartitionSpec as P

HEADS = 8
HSIZE = 112
TOK = 192
CLIP_MAX = 128
FEAT = 896
NZ, NCORE, NY, NX = 8, 2, 8, 8
ROWS = 14
COLS = 56
SCALE = HSIZE ** (-0.5)
TILE = 128
VMEM_BYTES = 14 * 1024 * 1024

Y_GROUPS = [[y * NX + x for y in range(NY)] for x in range(NX)]
X_GROUPS = [[y * NX + x for x in range(NX)] for y in range(NY)]
PLANE_GROUPS = [
    [(z * NCORE + c) * NY * NX + y * NX + x for z in range(NZ) for y in range(NY)]
    for c in range(NCORE)
    for x in range(NX)
]
NT = (((1,), (1,)), ((), ()))
NN = (((1,), (0,)), ((), ()))
TN = (((0,), (0,)), ((), ()))


def dot(a, b, dims):
    return lax.dot_general(a, b, dims, preferred_element_type=jnp.float32)


def window(head):
    low = HSIZE * head
    start = TILE * (low // TILE)
    stop = TILE * (-(-(low + HSIZE) // TILE))
    return start, stop


def own_lanes(head):
    start, stop = window(head)
    lane = lax.broadcasted_iota(jnp.int32, (1, stop - start), 1) + start
    return (lane >= HSIZE * head) & (lane < HSIZE * (head + 1))


def gathered_lanes(width):
    row = lax.broadcasted_iota(jnp.int32, (TILE, width), 0)
    lane = lax.broadcasted_iota(jnp.int32, (TILE, width), 1)
    inner = row & 15
    return jnp.where(inner < ROWS, lane - (row >> 4) * ROWS - inner, -1)


def kept(mask, value):
    return jnp.where(mask, value, jnp.zeros((), value.dtype))


def as_bf16(mask):
    return mask.astype(jnp.float32).astype(jnp.bfloat16)


def clip_ends(len_ref, rank):
    first = len_ref[0, 0, rank]
    return first, first + len_ref[1, 0, rank]


def moved_clip(len_ref, move_ref, source):
    first, second = clip_ends(len_ref, source)
    begin = jnp.int32(0)
    count = jnp.int32(0)
    for step in range(move_ref.shape[0]):
        mine = move_ref[step, 0] == source
        clip = move_ref[step, 2]
        clip_begin = jnp.where(clip == 0, 0, jnp.where(clip == 1, first, second))
        clip_end = jnp.where(clip == 0, first, jnp.where(clip == 1, second, TOK))
        begin = jnp.where(mine, clip_begin, begin)
        count = jnp.where(mine, clip_end - clip_begin, count)
    return begin, count


def attention(query, key, allowed):
    scores = dot(query, key, NT) * SCALE
    scores = jnp.where(allowed, scores, -1000000000.0)
    peak = jnp.max(scores, axis=1, keepdims=True)
    grown = jnp.exp(scores - peak)
    return grown * (1.0 / jnp.sum(grown, axis=1, keepdims=True))


def pack_body(len_ref, move_ref, qkv_ref, cot_ref, box_ref):
    rank = lax.axis_index("dp")
    begin, count = moved_clip(len_ref, move_ref, rank)
    row = lax.broadcasted_iota(jnp.int32, (CLIP_MAX, TOK), 0)
    col = lax.broadcasted_iota(jnp.int32, (CLIP_MAX, TOK), 1)
    pick = as_bf16((col == row + begin) & (row < count))
    for which in range(3):
        box_ref[which] = dot(pick, qkv_ref[which], NN).astype(jnp.bfloat16)
    box_ref[3] = dot(pick, cot_ref[...], NN).astype(jnp.bfloat16)


def box_body(len_ref, move_ref, box_ref, prob_ref):
    rank = lax.axis_index("dp")
    _, count = moved_clip(len_ref, move_ref, rank)
    row = lax.broadcasted_iota(jnp.int32, (CLIP_MAX, CLIP_MAX), 0)
    col = lax.broadcasted_iota(jnp.int32, (CLIP_MAX, CLIP_MAX), 1)
    for head in range(HEADS):
        start, stop = window(head)
        query = kept(own_lanes(head), box_ref[0, :, start:stop])
        probs = attention(query, box_ref[1, :, start:stop], col < count)
        prob_ref[head] = jnp.where(row < count, probs, 0.0).astype(jnp.bfloat16)


def forward_body(
    len_ref, qkv_ref, cot_ref, own_ref, other_ref, prob_ref, token_ref, mix_ref, term_ref,
):
    rank = lax.axis_index("dp")
    first, second = clip_ends(len_ref, rank)

    def segment(shape, dim):
        place = lax.broadcasted_iota(jnp.int32, shape, dim)
        return (place >= first).astype(jnp.int32) + (place >= second).astype(jnp.int32)

    allowed = segment((TOK, TOK), 0) == segment((TOK, TOK), 1)
    for head in range(HEADS):
        start, stop = window(head)
        lanes = own_lanes(head)
        query = kept(lanes, qkv_ref[0, :, start:stop])
        value = kept(lanes, qkv_ref[2, :, start:stop])
        probs = attention(query, qkv_ref[1, :, start:stop], allowed).astype(jnp.bfloat16)
        prob_ref[head] = probs
        mixed = dot(probs, value, NN)
        offset = HSIZE * head - start
        if offset:
            mixed = pltpu.roll(mixed, stop - start - offset, 1)
        mix_ref[:, head * TILE:(head + 1) * TILE] = mixed[:, :TILE].astype(jnp.bfloat16)

    term_ref[...] = dot(cot_ref[...], mix_ref[...], TN)
    core = lax.rem(rank, NCORE)
    for z in range(NZ):
        for ref, part in ((own_ref, core), (other_ref, 1 - core)):
            rows = pl.ds(pl.multiple_of(2 * COLS * z + COLS * part, 8), COLS)
            for y in range(NY):
                ref[z * NY + y] = term_ref[rows, y * TILE:(y + 1) * TILE].astype(jnp.bfloat16)
    token_ref[...] = jnp.zeros(token_ref.shape, jnp.float32)


class Tiles:
    def __init__(self, ref, mask):
        self.ref = ref
        self.mask = mask
        self.held = [[None] * (FEAT // TILE) for _ in range(3)]

    def add(self, which, head, part):
        start, stop = window(head)
        for tile in range(start // TILE, stop // TILE):
            piece = part[:, tile * TILE - start:(tile + 1) * TILE - start]
            held = self.held[which][tile]
            held = piece if held is None else held + piece
            self.held[which][tile] = held
            if HSIZE * (head + 1) >= TILE * (tile + 1):
                if self.mask is not None:
                    held = jnp.where(self.mask, held, 0.0)
                self.ref[which, :, tile * TILE:(tile + 1) * TILE] = held.astype(jnp.bfloat16)


def add_gradient(tiles, head, rows_ref, probs, back):
    start, stop = window(head)
    lanes = own_lanes(head)
    query = kept(lanes, rows_ref[0, :, start:stop])
    key = kept(lanes, rows_ref[1, :, start:stop])
    grad_p = dot(back, rows_ref[2, :, start:stop], NT)
    wide = probs.astype(jnp.float32)
    weighted = wide * grad_p
    grad_s = weighted - wide * jnp.sum(weighted, axis=1, keepdims=True)
    grad_s = (grad_s * SCALE).astype(jnp.bfloat16)
    tiles.add(0, head, dot(grad_s, key, NN))
    tiles.add(1, head, dot(grad_s, query, TN))
    tiles.add(2, head, dot(probs, back, TN))


def back_window(head, cot, weight_ref):
    start, stop = window(head)
    packed = dot(cot, weight_ref[:, head].reshape(TILE, FEAT), NT).astype(jnp.bfloat16)
    pick = as_bf16(gathered_lanes(stop - start) == HSIZE * head - start)
    return dot(packed, pick, NN).astype(jnp.bfloat16)


def box_backward_body(box_ref, prob_ref, weight_ref, send_ref, token_ref):
    tiles = Tiles(send_ref, None)
    cot = box_ref[3]
    for head in range(HEADS):
        add_gradient(tiles, head, box_ref, prob_ref[head], back_window(head, cot, weight_ref))
    token_ref[...] = jnp.zeros(token_ref.shape, jnp.float32)


def home_backward_body(
    len_ref, move_ref, qkv_ref, cot_ref, prob_ref, weight_ref, order_ref, home_ref, token_ref,
):
    rank = lax.axis_index("dp")
    begin, count = moved_clip(len_ref, move_ref, rank)
    place = lax.broadcasted_iota(jnp.int32, (TOK, TILE), 0)
    tiles = Tiles(home_ref, (place < begin) | (place >= begin + count))
    cot = cot_ref[...]
    for head in range(HEADS):
        add_gradient(tiles, head, qkv_ref, prob_ref[head], back_window(head, cot, weight_ref))
    token_ref[...] = order_ref[...]


def copies_body(shard_ref, copies_ref):
    shard = shard_ref[...].astype(jnp.float32)
    shard = jnp.concatenate([shard, jnp.zeros((16 - ROWS, FEAT), jnp.float32)], axis=0)
    shard = shard.astype(jnp.bfloat16)
    for y in range(NY):
        copies_ref[y] = shard


def plane_body(got_ref, out_ref, turned_ref):
    total = jnp.sum(got_ref[...].astype(jnp.float32), axis=0)
    total = jnp.concatenate([total, jnp.zeros((TILE - COLS, TILE), jnp.float32)], axis=0)
    turned_ref[...] = jnp.transpose(total)
    out_ref[...] = jnp.zeros(out_ref.shape, jnp.float32)
    for x in range(NX):
        for b in range(2):
            rows = turned_ref[pl.ds(ROWS * x + b, ROWS // 2, stride=2), :]
            out_ref[x, :ROWS // 2, b * COLS:(b + 1) * COLS] = rows[:, :COLS]


def row_body(got_ref, order_ref, out_ref):
    total = jnp.sum(got_ref[...], axis=0)
    for b in range(2):
        out_ref[pl.ds(b, ROWS // 2, stride=2), :] = total[:ROWS // 2, b * COLS:(b + 1) * COLS]


def in_vmem():
    return pl.BlockSpec(memory_space=pltpu.VMEM)


def in_smem():
    return pl.BlockSpec(memory_space=pltpu.SMEM)


def shape_of(shape, dtype):
    return jax.ShapeDtypeStruct(shape, dtype)


TOKEN = shape_of((8, TILE), jnp.float32)


def kernel(body, name, outs, scalars, arrays, scratch=(), flops=100_000_000):
    return pl.pallas_call(
        body,
        out_shape=outs,
        in_specs=[in_smem()] * len(scalars) + [in_vmem()] * len(arrays),
        out_specs=tuple(in_vmem() for _ in outs),
        scratch_shapes=list(scratch),
        compiler_params=pltpu.CompilerParams(vmem_limit_bytes=VMEM_BYTES),
        cost_estimate=pl.CostEstimate(flops=flops, bytes_accessed=4_000_000, transcendentals=0),
        name=name,
    )(*scalars, *arrays)


def after(value, *others):
    return lax.optimization_barrier((value,) + others)[0]


def local(qkv, grad_out, lengths, moves, out_weight):
    rows = jnp.transpose(qkv[0, 0], (1, 0, 2))
    cot = grad_out[0, 0]
    counts = jnp.transpose(lengths, (2, 1, 0))
    moving = moves[0]
    ranks = NZ * NCORE
    bf16 = jnp.bfloat16

    with jax.named_scope("weights_y"):
        (copies,) = kernel(
            copies_body, "copies", (shape_of((NY, 16, FEAT), bf16),), (), (out_weight,)
        )
        column = lax.all_to_all(copies, "fsdp", 0, 0, tiled=True, axis_index_groups=Y_GROUPS)

    own, other, probs, token = kernel(
        forward_body,
        "forward",
        (
            shape_of((NZ * NY, COLS, TILE), bf16),
            shape_of((NZ * NY, COLS, TILE), bf16),
            shape_of((HEADS, TOK, TOK), bf16),
            TOKEN,
        ),
        (counts,),
        (rows, cot),
        scratch=(
            pltpu.VMEM((TOK, HEADS * TILE), bf16),
            pltpu.VMEM((FEAT, HEADS * TILE), jnp.float32),
        ),
        flops=3_000_000_000,
    )
    column = after(column, token)
    with jax.named_scope("weights_x"):
        weights = lax.all_gather(
            column.reshape(NY * 16, FEAT), "fsdp", axis=0, tiled=True, axis_index_groups=X_GROUPS
        )
    swapped = lax.ppermute(other, "dp", [(i, i + 1 - 2 * (i % NCORE)) for i in range(ranks)])
    pair = (own.astype(jnp.float32) + swapped.astype(jnp.float32)).astype(bf16)
    with jax.named_scope("reduce_zy"):
        got = lax.all_to_all(
            pair, ("dp", "fsdp"), 0, 0, tiled=True, axis_index_groups=PLANE_GROUPS
        )

    later = after(counts, token)
    (box,) = kernel(
        pack_body, "pack", (shape_of((4, CLIP_MAX, FEAT), bf16),), (later, moving), (rows, cot)
    )
    (box_probs,) = kernel(
        box_body, "box_forward", (shape_of((HEADS, CLIP_MAX, CLIP_MAX), bf16),),
        (later, moving), (box,), flops=1_000_000_000,
    )

    (plane,) = kernel(
        plane_body, "plane_sum", (shape_of((NX, 8, TILE), jnp.float32),), (), (got,),
        scratch=(pltpu.VMEM((TILE, TILE), jnp.float32),),
    )
    with jax.named_scope("reduce_x"):
        parts = lax.all_to_all(plane, "fsdp", 0, 0, tiled=True, axis_index_groups=X_GROUPS)
    weights = after(weights, plane).reshape(NX, NY, 16, FEAT)
    send, token = kernel(
        box_backward_body, "box_backward", (shape_of((3, CLIP_MAX, FEAT), bf16), TOKEN), (),
        (box, box_probs, weights), flops=3_000_000_000,
    )
    inbox = lax.ppermute(send, "dp", [(i, (i + 1) % ranks) for i in range(ranks)])
    home, token = kernel(
        home_backward_body, "home_backward", (shape_of((3, TOK, FEAT), bf16), TOKEN),
        (counts, moving), (rows, cot, probs, weights, token), flops=6_000_000_000,
    )
    (weight_grad,) = kernel(
        row_body, "row_sum", (shape_of((ROWS, COLS), jnp.float32),), (), (parts, token)
    )
    return (
        jnp.transpose(home, (1, 0, 2))[None, None],
        jnp.transpose(inbox, (1, 0, 2))[None, None],
        weight_grad,
    )


def solution(mesh):
    placed = (
        P("dp", "fsdp", None, None, None),
        P("dp", "fsdp", None, None),
        P(None, "fsdp", None),
        P("fsdp", None, None),
        P("fsdp", None),
    )
    return jax.shard_map(
        local,
        mesh=mesh,
        in_specs=placed,
        out_specs=(
            P("dp", "fsdp", None, None, None),
            P("dp", "fsdp", None, None, None),
            P("fsdp", "dp"),
        ),
        check_vma=False,
    )
```

```python
import jax
import jax.numpy as jnp
import numpy as np
from jax import lax
from jax.experimental import pallas as pl
from jax.experimental.pallas import tpu as pltpu
from jax.sharding import PartitionSpec as P

HEADS = 8
HSIZE = 112
TOK = 192
CLIP_MAX = 128
FEAT = 896
NZ, NCORE, NY, NX = 8, 2, 8, 8
ROWS = 14
COLS = 56
SCALE = HSIZE ** (-0.5)
TILE = 128
SMALL_GRANT = 14 * 1024 * 1024
LARGE_GRANT = 60 * 1024 * 1024

Y_GROUPS = [[y * NX + x for y in range(NY)] for x in range(NX)]
X_GROUPS = [[y * NX + x for x in range(NX)] for y in range(NY)]
PLANE_GROUPS = [
    [(z * NCORE + c) * NY * NX + y * NX + x for z in range(NZ) for y in range(NY)]
    for c in range(NCORE)
    for x in range(NX)
]
NT = (((1,), (1,)), ((), ()))
NN = (((1,), (0,)), ((), ()))
TN = (((0,), (0,)), ((), ()))


def dot(a, b, dims):
    return lax.dot_general(a, b, dims, preferred_element_type=jnp.float32)


def window(head):
    low = HSIZE * head
    start = TILE * (low // TILE)
    stop = TILE * (-(-(low + HSIZE) // TILE))
    return start, stop


def own_lanes(head):
    start, stop = window(head)
    lane = lax.broadcasted_iota(jnp.int32, (1, stop - start), 1) + start
    return (lane >= HSIZE * head) & (lane < HSIZE * (head + 1))


def gathered_lanes(width):
    row = lax.broadcasted_iota(jnp.int32, (TILE, width), 0)
    lane = lax.broadcasted_iota(jnp.int32, (TILE, width), 1)
    inner = row & 15
    return jnp.where(inner < ROWS, lane - (row >> 4) * ROWS - inner, -1)


def kept(mask, value):
    return jnp.where(mask, value, jnp.zeros((), value.dtype))


def as_bf16(mask):
    return mask.astype(jnp.float32).astype(jnp.bfloat16)


def clip_ends(len_ref, rank):
    first = len_ref[0, 0, rank]
    return first, first + len_ref[1, 0, rank]


def moved_clip(len_ref, move_ref, source):
    first, second = clip_ends(len_ref, source)
    begin = jnp.int32(0)
    count = jnp.int32(0)
    for step in range(move_ref.shape[0]):
        mine = move_ref[step, 0] == source
        clip = move_ref[step, 2]
        clip_begin = jnp.where(clip == 0, 0, jnp.where(clip == 1, first, second))
        clip_end = jnp.where(clip == 0, first, jnp.where(clip == 1, second, TOK))
        begin = jnp.where(mine, clip_begin, begin)
        count = jnp.where(mine, clip_end - clip_begin, count)
    return begin, count


def attention(query, key, allowed):
    scores = dot(query, key, NT) * SCALE
    scores = jnp.where(allowed, scores, -1000000000.0)
    peak = jnp.max(scores, axis=1, keepdims=True)
    grown = jnp.exp(scores - peak)
    return grown * (1.0 / jnp.sum(grown, axis=1, keepdims=True))


def pack_body(len_ref, move_ref, qkv_ref, cot_ref, box_ref):
    rank = lax.axis_index("dp")
    begin, count = moved_clip(len_ref, move_ref, rank)
    row = lax.broadcasted_iota(jnp.int32, (CLIP_MAX, TOK), 0)
    col = lax.broadcasted_iota(jnp.int32, (CLIP_MAX, TOK), 1)
    pick = as_bf16((col == row + begin) & (row < count))
    for which in range(3):
        box_ref[which] = dot(pick, qkv_ref[which], NN).astype(jnp.bfloat16)
    box_ref[3] = dot(pick, cot_ref[...], NN).astype(jnp.bfloat16)


def box_body(len_ref, move_ref, box_ref, prob_ref):
    rank = lax.axis_index("dp")
    _, count = moved_clip(len_ref, move_ref, rank)
    row = lax.broadcasted_iota(jnp.int32, (CLIP_MAX, CLIP_MAX), 0)
    col = lax.broadcasted_iota(jnp.int32, (CLIP_MAX, CLIP_MAX), 1)
    for head in range(HEADS):
        start, stop = window(head)
        query = kept(own_lanes(head), box_ref[0, :, start:stop])
        probs = attention(query, box_ref[1, :, start:stop], col < count)
        prob_ref[head] = jnp.where(row < count, probs, 0.0).astype(jnp.bfloat16)


def forward_body(
    len_ref, qkv_ref, cot_ref, own_ref, other_ref, prob_ref, token_ref, mix_ref, term_ref,
):
    rank = lax.axis_index("dp")
    first, second = clip_ends(len_ref, rank)

    def segment(shape, dim):
        place = lax.broadcasted_iota(jnp.int32, shape, dim)
        return (place >= first).astype(jnp.int32) + (place >= second).astype(jnp.int32)

    allowed = segment((TOK, TOK), 0) == segment((TOK, TOK), 1)
    for head in range(HEADS):
        start, stop = window(head)
        lanes = own_lanes(head)
        query = kept(lanes, qkv_ref[0, :, start:stop])
        value = kept(lanes, qkv_ref[2, :, start:stop])
        probs = attention(query, qkv_ref[1, :, start:stop], allowed).astype(jnp.bfloat16)
        prob_ref[head] = probs
        mixed = dot(probs, value, NN)
        offset = HSIZE * head - start
        if offset:
            mixed = pltpu.roll(mixed, stop - start - offset, 1)
        mix_ref[:, head * TILE:(head + 1) * TILE] = mixed[:, :TILE].astype(jnp.bfloat16)

    term_ref[...] = dot(cot_ref[...], mix_ref[...], TN)
    core = lax.rem(rank, NCORE)
    for z in range(NZ):
        for ref, part in ((own_ref, core), (other_ref, 1 - core)):
            rows = pl.ds(pl.multiple_of(2 * COLS * z + COLS * part, 8), COLS)
            for y in range(NY):
                ref[z * NY + y] = term_ref[rows, y * TILE:(y + 1) * TILE].astype(jnp.bfloat16)
    token_ref[...] = jnp.zeros(token_ref.shape, jnp.float32)


class Tiles:
    def __init__(self, ref, mask):
        self.ref = ref
        self.mask = mask
        self.held = [[None] * (FEAT // TILE) for _ in range(3)]

    def add(self, which, head, part):
        start, stop = window(head)
        for tile in range(start // TILE, stop // TILE):
            piece = part[:, tile * TILE - start:(tile + 1) * TILE - start]
            held = self.held[which][tile]
            held = piece if held is None else held + piece
            self.held[which][tile] = held
            if HSIZE * (head + 1) >= TILE * (tile + 1):
                if self.mask is not None:
                    held = jnp.where(self.mask, held, 0.0)
                self.ref[which, :, tile * TILE:(tile + 1) * TILE] = held.astype(jnp.bfloat16)


def add_gradient(tiles, head, rows_ref, probs, back):
    start, stop = window(head)
    lanes = own_lanes(head)
    query = kept(lanes, rows_ref[0, :, start:stop])
    key = kept(lanes, rows_ref[1, :, start:stop])
    grad_p = dot(back, rows_ref[2, :, start:stop], NT)
    wide = probs.astype(jnp.float32)
    weighted = wide * grad_p
    grad_s = weighted - wide * jnp.sum(weighted, axis=1, keepdims=True)
    grad_s = (grad_s * SCALE).astype(jnp.bfloat16)
    tiles.add(0, head, dot(grad_s, key, NN))
    tiles.add(1, head, dot(grad_s, query, TN))
    tiles.add(2, head, dot(probs, back, TN))


def weight_copy(head, weight_ref, held_ref, sem):
    return pltpu.make_async_copy(weight_ref.at[:, head], held_ref.at[head], sem.at[head])


def back_window(head, cot, weights):
    start, stop = window(head)
    packed = dot(cot, weights.reshape(TILE, FEAT), NT).astype(jnp.bfloat16)
    pick = as_bf16(gathered_lanes(stop - start) == HSIZE * head - start)
    return dot(packed, pick, NN).astype(jnp.bfloat16)


def all_gradients(tiles, rows_ref, cot, prob_ref, weight_ref, held_ref, sem):
    for head in range(HEADS):
        weight_copy(head, weight_ref, held_ref, sem).start()
    for head in range(HEADS):
        weight_copy(head, weight_ref, held_ref, sem).wait()
        back = back_window(head, cot, held_ref[head])
        add_gradient(tiles, head, rows_ref, prob_ref[head], back)


def box_backward_body(box_ref, prob_ref, weight_ref, send_ref, token_ref, held_ref, sem):
    tiles = Tiles(send_ref, None)
    all_gradients(tiles, box_ref, box_ref[3], prob_ref, weight_ref, held_ref, sem)
    token_ref[...] = jnp.zeros(token_ref.shape, jnp.float32)


def home_backward_body(
    len_ref, move_ref, qkv_ref, cot_ref, prob_ref, order_ref, weight_ref,
    home_ref, token_ref, held_ref, sem,
):
    rank = lax.axis_index("dp")
    begin, count = moved_clip(len_ref, move_ref, rank)
    place = lax.broadcasted_iota(jnp.int32, (TOK, TILE), 0)
    tiles = Tiles(home_ref, (place < begin) | (place >= begin + count))
    all_gradients(tiles, qkv_ref, cot_ref[...], prob_ref, weight_ref, held_ref, sem)
    token_ref[...] = order_ref[...]


def copies_body(shard_ref, copies_ref):
    shard = shard_ref[...].astype(jnp.float32)
    shard = jnp.concatenate([shard, jnp.zeros((16 - ROWS, FEAT), jnp.float32)], axis=0)
    shard = shard.astype(jnp.bfloat16)
    for y in range(NY):
        copies_ref[y] = shard


def plane_body(got_ref, out_ref, turned_ref):
    total = jnp.sum(got_ref[...].astype(jnp.float32), axis=0)
    total = jnp.concatenate([total, jnp.zeros((TILE - COLS, TILE), jnp.float32)], axis=0)
    turned_ref[...] = jnp.transpose(total)
    out_ref[...] = jnp.zeros(out_ref.shape, jnp.float32)
    for x in range(NX):
        for b in range(2):
            rows = turned_ref[pl.ds(ROWS * x + b, ROWS // 2, stride=2), :]
            out_ref[x, :ROWS // 2, b * COLS:(b + 1) * COLS] = rows[:, :COLS]


def row_body(got_ref, order_ref, out_ref):
    total = jnp.sum(got_ref[...], axis=0)
    for b in range(2):
        out_ref[pl.ds(b, ROWS // 2, stride=2), :] = total[:ROWS // 2, b * COLS:(b + 1) * COLS]


def in_vmem():
    return pl.BlockSpec(memory_space=pltpu.VMEM)


def in_smem():
    return pl.BlockSpec(memory_space=pltpu.SMEM)


def shape_of(shape, dtype):
    return jax.ShapeDtypeStruct(shape, dtype)


TOKEN = shape_of((8, TILE), jnp.float32)


def kernel(
    body, name, outs, scalars, arrays, far=(), scratch=(), flops=100_000_000, grant=LARGE_GRANT
):
    return pl.pallas_call(
        body,
        out_shape=outs,
        in_specs=[in_smem()] * len(scalars)
        + [in_vmem()] * len(arrays)
        + [pl.BlockSpec(memory_space=pltpu.HBM)] * len(far),
        out_specs=tuple(in_vmem() for _ in outs),
        scratch_shapes=list(scratch),
        compiler_params=pltpu.CompilerParams(vmem_limit_bytes=grant),
        cost_estimate=pl.CostEstimate(flops=flops, bytes_accessed=flops // 100, transcendentals=0),
        name=name,
    )(*scalars, *arrays, *far)


def after(value, *others):
    return lax.optimization_barrier((value,) + others)[0]


def local(qkv, grad_out, lengths, moves, out_weight):
    rows = jnp.transpose(qkv[0, 0], (1, 0, 2))
    cot = grad_out[0, 0]
    counts = jnp.transpose(lengths, (2, 1, 0))
    moving = moves[0]
    ranks = NZ * NCORE
    bf16 = jnp.bfloat16

    with jax.named_scope("weights_y"):
        (copies,) = kernel(
            copies_body, "copies", (shape_of((NY, 16, FEAT), bf16),), (), (out_weight,)
        )
        column = lax.all_to_all(copies, "fsdp", 0, 0, tiled=True, axis_index_groups=Y_GROUPS)

    own, other, probs, token = kernel(
        forward_body,
        "forward",
        (
            shape_of((NZ * NY, COLS, TILE), bf16),
            shape_of((NZ * NY, COLS, TILE), bf16),
            shape_of((HEADS, TOK, TOK), bf16),
            TOKEN,
        ),
        (counts,),
        (rows, cot),
        scratch=(
            pltpu.VMEM((TOK, HEADS * TILE), bf16),
            pltpu.VMEM((FEAT, HEADS * TILE), jnp.float32),
        ),
        flops=3_000_000_000,
    )
    column = after(column, token)
    with jax.named_scope("weights_x"):
        weights = lax.all_gather(
            column.reshape(NY * 16, FEAT), "fsdp", axis=0, tiled=True, axis_index_groups=X_GROUPS
        )
    swapped = lax.ppermute(other, "dp", [(i, i + 1 - 2 * (i % NCORE)) for i in range(ranks)])
    pair = (own.astype(jnp.float32) + swapped.astype(jnp.float32)).astype(bf16)
    with jax.named_scope("reduce_zy"):
        got = lax.all_to_all(
            pair, ("dp", "fsdp"), 0, 0, tiled=True, axis_index_groups=PLANE_GROUPS
        )

    later = after(counts, token)
    (box,) = kernel(
        pack_body, "pack", (shape_of((4, CLIP_MAX, FEAT), bf16),), (later, moving), (rows, cot)
    )
    (box_probs,) = kernel(
        box_body, "box_forward", (shape_of((HEADS, CLIP_MAX, CLIP_MAX), bf16),),
        (later, moving), (box,), flops=1_000_000_000,
    )

    (plane,) = kernel(
        plane_body, "plane_sum", (shape_of((NX, 8, TILE), jnp.float32),), (), (got,),
        scratch=(pltpu.VMEM((TILE, TILE), jnp.float32),), grant=SMALL_GRANT,
    )
    with jax.named_scope("reduce_x"):
        parts = lax.all_to_all(plane, "fsdp", 0, 0, tiled=True, axis_index_groups=X_GROUPS)
    weights = after(weights, plane).reshape(NX, NY, 16, FEAT)
    held = (
        pltpu.VMEM((HEADS, NX, 16, FEAT), bf16),
        pltpu.SemaphoreType.DMA((HEADS,)),
    )
    send, token = kernel(
        box_backward_body, "box_backward", (shape_of((3, CLIP_MAX, FEAT), bf16), TOKEN), (),
        (box, box_probs), far=(weights,), scratch=held, flops=1000,
    )
    inbox = lax.ppermute(send, "dp", [(i, (i + 1) % ranks) for i in range(ranks)])
    home, token = kernel(
        home_backward_body, "home_backward", (shape_of((3, TOK, FEAT), bf16), TOKEN),
        (counts, moving), (rows, cot, probs, token), far=(weights,), scratch=held, flops=1000,
    )
    (weight_grad,) = kernel(
        row_body, "row_sum", (shape_of((ROWS, COLS), jnp.float32),), (), (parts, token),
        grant=SMALL_GRANT,
    )
    return (
        jnp.transpose(home, (1, 0, 2))[None, None],
        jnp.transpose(inbox, (1, 0, 2))[None, None],
        weight_grad,
    )


def solution(mesh):
    placed = (
        P("dp", "fsdp", None, None, None),
        P("dp", "fsdp", None, None),
        P(None, "fsdp", None),
        P("fsdp", None, None),
        P("fsdp", None),
    )
    return jax.shard_map(
        local,
        mesh=mesh,
        in_specs=placed,
        out_specs=(
            P("dp", "fsdp", None, None, None),
            P("dp", "fsdp", None, None, None),
            P("fsdp", "dp"),
        ),
        check_vma=False,
    )
```

```python
import jax
import jax.numpy as jnp
import numpy as np
from jax import lax
from jax.experimental import pallas as pl
from jax.experimental.pallas import tpu as pltpu
from jax.sharding import PartitionSpec as P

HEADS = 8
HSIZE = 112
TOK = 192
CLIP_MAX = 128
FEAT = 896
NZ, NCORE, NY, NX = 8, 2, 8, 8
ROWS = 14
COLS = 56
SCALE = HSIZE ** (-0.5)
TILE = 128
VMEM_BYTES = 14 * 1024 * 1024

Y_GROUPS = [[y * NX + x for y in range(NY)] for x in range(NX)]
X_GROUPS = [[y * NX + x for x in range(NX)] for y in range(NY)]
PLANE_GROUPS = [
    [(z * NCORE + c) * NY * NX + y * NX + x for z in range(NZ) for y in range(NY)]
    for c in range(NCORE)
    for x in range(NX)
]
NT = (((1,), (1,)), ((), ()))
NN = (((1,), (0,)), ((), ()))
TN = (((0,), (0,)), ((), ()))


def dot(a, b, dims):
    return lax.dot_general(a, b, dims, preferred_element_type=jnp.float32)


def window(head):
    low = HSIZE * head
    start = TILE * (low // TILE)
    stop = TILE * (-(-(low + HSIZE) // TILE))
    return start, stop


def own_lanes(head):
    start, stop = window(head)
    lane = lax.broadcasted_iota(jnp.int32, (1, stop - start), 1) + start
    return (lane >= HSIZE * head) & (lane < HSIZE * (head + 1))


def gathered_lanes(width):
    row = lax.broadcasted_iota(jnp.int32, (TILE, width), 0)
    lane = lax.broadcasted_iota(jnp.int32, (TILE, width), 1)
    inner = row & 15
    return jnp.where(inner < ROWS, lane - (row >> 4) * ROWS - inner, -1)


def kept(mask, value):
    return jnp.where(mask, value, jnp.zeros((), value.dtype))


def as_bf16(mask):
    return mask.astype(jnp.float32).astype(jnp.bfloat16)


def clip_ends(len_ref, rank):
    first = len_ref[0, 0, rank]
    return first, first + len_ref[1, 0, rank]


def moved_clip(len_ref, move_ref, source):
    first, second = clip_ends(len_ref, source)
    begin = jnp.int32(0)
    count = jnp.int32(0)
    for step in range(move_ref.shape[0]):
        mine = move_ref[step, 0] == source
        clip = move_ref[step, 2]
        clip_begin = jnp.where(clip == 0, 0, jnp.where(clip == 1, first, second))
        clip_end = jnp.where(clip == 0, first, jnp.where(clip == 1, second, TOK))
        begin = jnp.where(mine, clip_begin, begin)
        count = jnp.where(mine, clip_end - clip_begin, count)
    return begin, count


def attention(query, key, allowed):
    scores = dot(key, query, NT) * SCALE
    scores = jnp.where(allowed, scores, -1000000000.0)
    peak = jnp.max(scores, axis=0, keepdims=True)
    grown = jnp.exp(scores - peak)
    return grown * (1.0 / jnp.sum(grown, axis=0, keepdims=True))


def pack_body(len_ref, move_ref, qkv_ref, cot_ref, box_ref):
    rank = lax.axis_index("dp")
    begin, count = moved_clip(len_ref, move_ref, rank)
    row = lax.broadcasted_iota(jnp.int32, (CLIP_MAX, TOK), 0)
    col = lax.broadcasted_iota(jnp.int32, (CLIP_MAX, TOK), 1)
    pick = as_bf16((col == row + begin) & (row < count))
    for which in range(3):
        box_ref[which] = dot(pick, qkv_ref[which], NN).astype(jnp.bfloat16)
    box_ref[3] = dot(pick, cot_ref[...], NN).astype(jnp.bfloat16)


def box_body(len_ref, move_ref, box_ref, prob_ref):
    rank = lax.axis_index("dp")
    _, count = moved_clip(len_ref, move_ref, rank)
    row = lax.broadcasted_iota(jnp.int32, (CLIP_MAX, CLIP_MAX), 0)
    col = lax.broadcasted_iota(jnp.int32, (CLIP_MAX, CLIP_MAX), 1)
    for head in range(HEADS):
        start, stop = window(head)
        query = kept(own_lanes(head), box_ref[0, :, start:stop])
        probs = attention(query, box_ref[1, :, start:stop], row < count)
        prob_ref[head] = jnp.where(col < count, probs, 0.0).astype(jnp.bfloat16)


def forward_body(
    len_ref, qkv_ref, cot_ref, own_ref, other_ref, prob_ref, token_ref, mix_ref, term_ref,
):
    rank = lax.axis_index("dp")
    first, second = clip_ends(len_ref, rank)

    def segment(shape, dim):
        place = lax.broadcasted_iota(jnp.int32, shape, dim)
        return (place >= first).astype(jnp.int32) + (place >= second).astype(jnp.int32)

    allowed = segment((TOK, TOK), 0) == segment((TOK, TOK), 1)
    for head in range(HEADS):
        start, stop = window(head)
        lanes = own_lanes(head)
        query = kept(lanes, qkv_ref[0, :, start:stop])
        value = kept(lanes, qkv_ref[2, :, start:stop])
        probs = attention(query, qkv_ref[1, :, start:stop], allowed).astype(jnp.bfloat16)
        prob_ref[head] = probs
        mixed = dot(probs, value, TN)
        offset = HSIZE * head - start
        if offset:
            mixed = pltpu.roll(mixed, stop - start - offset, 1)
        mix_ref[:, head * TILE:(head + 1) * TILE] = mixed[:, :TILE].astype(jnp.bfloat16)

    term_ref[...] = dot(cot_ref[...], mix_ref[...], TN)
    core = lax.rem(rank, NCORE)
    for z in range(NZ):
        for ref, part in ((own_ref, core), (other_ref, 1 - core)):
            rows = pl.ds(pl.multiple_of(2 * COLS * z + COLS * part, 8), COLS)
            for y in range(NY):
                ref[z * NY + y] = term_ref[rows, y * TILE:(y + 1) * TILE].astype(jnp.bfloat16)
    token_ref[...] = jnp.zeros(token_ref.shape, jnp.float32)


class Tiles:
    def __init__(self, ref, mask):
        self.ref = ref
        self.mask = mask
        self.held = [[None] * (FEAT // TILE) for _ in range(3)]

    def add(self, which, head, part):
        start, stop = window(head)
        for tile in range(start // TILE, stop // TILE):
            piece = part[:, tile * TILE - start:(tile + 1) * TILE - start]
            held = self.held[which][tile]
            held = piece if held is None else held + piece
            self.held[which][tile] = held
            if HSIZE * (head + 1) >= TILE * (tile + 1):
                if self.mask is not None:
                    held = jnp.where(self.mask, held, 0.0)
                self.ref[which, :, tile * TILE:(tile + 1) * TILE] = held.astype(jnp.bfloat16)


def add_gradient(tiles, head, rows_ref, probs, back):
    start, stop = window(head)
    lanes = own_lanes(head)
    query = kept(lanes, rows_ref[0, :, start:stop])
    key = kept(lanes, rows_ref[1, :, start:stop])
    grad_p = dot(rows_ref[2, :, start:stop], back, NT)
    wide = probs.astype(jnp.float32)
    weighted = wide * grad_p
    grad_s = weighted - wide * jnp.sum(weighted, axis=0, keepdims=True)
    grad_s = (grad_s * SCALE).astype(jnp.bfloat16)
    tiles.add(0, head, dot(grad_s, key, TN))
    tiles.add(1, head, dot(grad_s, query, NN))
    tiles.add(2, head, dot(probs, back, NN))


def back_window(head, cot, weight_ref):
    start, stop = window(head)
    packed = dot(cot, weight_ref[:, head].reshape(TILE, FEAT), NT).astype(jnp.bfloat16)
    pick = as_bf16(gathered_lanes(stop - start) == HSIZE * head - start)
    return dot(packed, pick, NN).astype(jnp.bfloat16)


def box_backward_body(box_ref, prob_ref, weight_ref, send_ref, token_ref):
    tiles = Tiles(send_ref, None)
    cot = box_ref[3]
    for head in range(HEADS):
        add_gradient(tiles, head, box_ref, prob_ref[head], back_window(head, cot, weight_ref))
    token_ref[...] = jnp.zeros(token_ref.shape, jnp.float32)


def home_backward_body(
    len_ref, move_ref, qkv_ref, cot_ref, prob_ref, weight_ref, order_ref, home_ref, token_ref,
):
    rank = lax.axis_index("dp")
    begin, count = moved_clip(len_ref, move_ref, rank)
    place = lax.broadcasted_iota(jnp.int32, (TOK, TILE), 0)
    tiles = Tiles(home_ref, (place < begin) | (place >= begin + count))
    cot = cot_ref[...]
    for head in range(HEADS):
        add_gradient(tiles, head, qkv_ref, prob_ref[head], back_window(head, cot, weight_ref))
    token_ref[...] = order_ref[...]


def copies_body(shard_ref, copies_ref):
    shard = shard_ref[...].astype(jnp.float32)
    shard = jnp.concatenate([shard, jnp.zeros((16 - ROWS, FEAT), jnp.float32)], axis=0)
    shard = shard.astype(jnp.bfloat16)
    for y in range(NY):
        copies_ref[y] = shard


def plane_body(got_ref, out_ref, turned_ref):
    total = jnp.sum(got_ref[...].astype(jnp.float32), axis=0)
    total = jnp.concatenate([total, jnp.zeros((TILE - COLS, TILE), jnp.float32)], axis=0)
    turned_ref[...] = jnp.transpose(total)
    out_ref[...] = jnp.zeros(out_ref.shape, jnp.float32)
    for x in range(NX):
        for b in range(2):
            rows = turned_ref[pl.ds(ROWS * x + b, ROWS // 2, stride=2), :]
            out_ref[x, :ROWS // 2, b * COLS:(b + 1) * COLS] = rows[:, :COLS]


def row_body(got_ref, order_ref, out_ref):
    total = jnp.sum(got_ref[...], axis=0)
    for b in range(2):
        out_ref[pl.ds(b, ROWS // 2, stride=2), :] = total[:ROWS // 2, b * COLS:(b + 1) * COLS]


def in_vmem():
    return pl.BlockSpec(memory_space=pltpu.VMEM)


def in_smem():
    return pl.BlockSpec(memory_space=pltpu.SMEM)


def shape_of(shape, dtype):
    return jax.ShapeDtypeStruct(shape, dtype)


TOKEN = shape_of((8, TILE), jnp.float32)


def kernel(body, name, outs, scalars, arrays, scratch=(), flops=100_000_000):
    return pl.pallas_call(
        body,
        out_shape=outs,
        in_specs=[in_smem()] * len(scalars) + [in_vmem()] * len(arrays),
        out_specs=tuple(in_vmem() for _ in outs),
        scratch_shapes=list(scratch),
        compiler_params=pltpu.CompilerParams(vmem_limit_bytes=VMEM_BYTES),
        cost_estimate=pl.CostEstimate(flops=flops, bytes_accessed=4_000_000, transcendentals=0),
        name=name,
    )(*scalars, *arrays)


def after(value, *others):
    return lax.optimization_barrier((value,) + others)[0]


def local(qkv, grad_out, lengths, moves, out_weight):
    rows = jnp.transpose(qkv[0, 0], (1, 0, 2))
    cot = grad_out[0, 0]
    counts = jnp.transpose(lengths, (2, 1, 0))
    moving = moves[0]
    ranks = NZ * NCORE
    bf16 = jnp.bfloat16

    with jax.named_scope("weights_y"):
        (copies,) = kernel(
            copies_body, "copies", (shape_of((NY, 16, FEAT), bf16),), (), (out_weight,)
        )
        column = lax.all_to_all(copies, "fsdp", 0, 0, tiled=True, axis_index_groups=Y_GROUPS)

    own, other, probs, token = kernel(
        forward_body,
        "forward",
        (
            shape_of((NZ * NY, COLS, TILE), bf16),
            shape_of((NZ * NY, COLS, TILE), bf16),
            shape_of((HEADS, TOK, TOK), bf16),
            TOKEN,
        ),
        (counts,),
        (rows, cot),
        scratch=(
            pltpu.VMEM((TOK, HEADS * TILE), bf16),
            pltpu.VMEM((FEAT, HEADS * TILE), jnp.float32),
        ),
        flops=3_000_000_000,
    )
    column = after(column, token)
    with jax.named_scope("weights_x"):
        weights = lax.all_gather(
            column.reshape(NY * 16, FEAT), "fsdp", axis=0, tiled=True, axis_index_groups=X_GROUPS
        )
    swapped = lax.ppermute(other, "dp", [(i, i + 1 - 2 * (i % NCORE)) for i in range(ranks)])
    pair = (own.astype(jnp.float32) + swapped.astype(jnp.float32)).astype(bf16)
    with jax.named_scope("reduce_zy"):
        got = lax.all_to_all(
            pair, ("dp", "fsdp"), 0, 0, tiled=True, axis_index_groups=PLANE_GROUPS
        )

    later = after(counts, token)
    (box,) = kernel(
        pack_body, "pack", (shape_of((4, CLIP_MAX, FEAT), bf16),), (later, moving), (rows, cot)
    )
    (box_probs,) = kernel(
        box_body, "box_forward", (shape_of((HEADS, CLIP_MAX, CLIP_MAX), bf16),),
        (later, moving), (box,), flops=1_000_000_000,
    )

    (plane,) = kernel(
        plane_body, "plane_sum", (shape_of((NX, 8, TILE), jnp.float32),), (), (got,),
        scratch=(pltpu.VMEM((TILE, TILE), jnp.float32),),
    )
    with jax.named_scope("reduce_x"):
        parts = lax.all_to_all(plane, "fsdp", 0, 0, tiled=True, axis_index_groups=X_GROUPS)
    weights = after(weights, plane).reshape(NX, NY, 16, FEAT)
    send, token = kernel(
        box_backward_body, "box_backward", (shape_of((3, CLIP_MAX, FEAT), bf16), TOKEN), (),
        (box, box_probs, weights), flops=3000000000,
    )
    inbox = lax.ppermute(send, "dp", [(i, (i + 1) % ranks) for i in range(ranks)])
    home, token = kernel(
        home_backward_body, "home_backward", (shape_of((3, TOK, FEAT), bf16), TOKEN),
        (counts, moving), (rows, cot, probs, weights, token), flops=12000000000,
    )
    (weight_grad,) = kernel(
        row_body, "row_sum", (shape_of((ROWS, COLS), jnp.float32),), (), (parts, token)
    )
    return (
        jnp.transpose(home, (1, 0, 2))[None, None],
        jnp.transpose(inbox, (1, 0, 2))[None, None],
        weight_grad,
    )


def solution(mesh):
    placed = (
        P("dp", "fsdp", None, None, None),
        P("dp", "fsdp", None, None),
        P(None, "fsdp", None),
        P("fsdp", None, None),
        P("fsdp", None),
    )
    return jax.shard_map(
        local,
        mesh=mesh,
        in_specs=placed,
        out_specs=(
            P("dp", "fsdp", None, None, None),
            P("dp", "fsdp", None, None, None),
            P("fsdp", "dp"),
        ),
        check_vma=False,
    )
```

```python
import jax
import jax.numpy as jnp
import numpy as np
from jax import lax
from jax.experimental import pallas as pl
from jax.experimental.pallas import tpu as pltpu
from jax.sharding import PartitionSpec as P

HEADS = 8
HSIZE = 112
TOK = 192
CLIP_MAX = 128
FEAT = 896
NZ, NCORE, NY, NX = 8, 2, 8, 8
ROWS = 14
COLS = 56
SCALE = HSIZE ** (-0.5)
TILE = 128
VMEM_BYTES = 14 * 1024 * 1024

Y_GROUPS = [[y * NX + x for y in range(NY)] for x in range(NX)]
X_GROUPS = [[y * NX + x for x in range(NX)] for y in range(NY)]
PLANE_GROUPS = [
    [(z * NCORE + c) * NY * NX + y * NX + x for z in range(NZ) for y in range(NY)]
    for c in range(NCORE)
    for x in range(NX)
]
NT = (((1,), (1,)), ((), ()))
NN = (((1,), (0,)), ((), ()))
TN = (((0,), (0,)), ((), ()))


def dot(a, b, dims):
    return lax.dot_general(a, b, dims, preferred_element_type=jnp.float32)


def window(head):
    low = HSIZE * head
    start = TILE * (low // TILE)
    stop = TILE * (-(-(low + HSIZE) // TILE))
    return start, stop


def own_lanes(head):
    start, stop = window(head)
    lane = lax.broadcasted_iota(jnp.int32, (1, stop - start), 1) + start
    return (lane >= HSIZE * head) & (lane < HSIZE * (head + 1))


def kept(mask, value):
    return jnp.where(mask, value, jnp.zeros((), value.dtype))


def as_bf16(mask):
    return mask.astype(jnp.float32).astype(jnp.bfloat16)


def clip_ends(len_ref, rank):
    first = len_ref[0, 0, rank]
    return first, first + len_ref[1, 0, rank]


def moved_clip(len_ref, move_ref, source):
    first, second = clip_ends(len_ref, source)
    begin = jnp.int32(0)
    count = jnp.int32(0)
    for step in range(move_ref.shape[0]):
        mine = move_ref[step, 0] == source
        clip = move_ref[step, 2]
        clip_begin = jnp.where(clip == 0, 0, jnp.where(clip == 1, first, second))
        clip_end = jnp.where(clip == 0, first, jnp.where(clip == 1, second, TOK))
        begin = jnp.where(mine, clip_begin, begin)
        count = jnp.where(mine, clip_end - clip_begin, count)
    return begin, count


def attention(query, key, allowed):
    scores = dot(key, query, NT) * SCALE
    scores = jnp.where(allowed, scores, -1000000000.0)
    peak = jnp.max(scores, axis=0, keepdims=True)
    grown = jnp.exp(scores - peak)
    return grown * (1.0 / jnp.sum(grown, axis=0, keepdims=True))


def pack_body(len_ref, move_ref, qkv_ref, cot_ref, box_ref):
    rank = lax.axis_index("dp")
    begin, count = moved_clip(len_ref, move_ref, rank)
    row = lax.broadcasted_iota(jnp.int32, (CLIP_MAX, TOK), 0)
    col = lax.broadcasted_iota(jnp.int32, (CLIP_MAX, TOK), 1)
    pick = as_bf16((col == row + begin) & (row < count))
    for which in range(3):
        box_ref[which] = dot(pick, qkv_ref[which], NN).astype(jnp.bfloat16)
    box_ref[3] = dot(pick, cot_ref[...], NN).astype(jnp.bfloat16)


def box_body(len_ref, move_ref, box_ref, prob_ref):
    rank = lax.axis_index("dp")
    _, count = moved_clip(len_ref, move_ref, rank)
    row = lax.broadcasted_iota(jnp.int32, (CLIP_MAX, CLIP_MAX), 0)
    col = lax.broadcasted_iota(jnp.int32, (CLIP_MAX, CLIP_MAX), 1)
    for head in range(HEADS):
        start, stop = window(head)
        query = kept(own_lanes(head), box_ref[0, :, start:stop])
        probs = attention(query, box_ref[1, :, start:stop], row < count)
        prob_ref[head] = jnp.where(col < count, probs, 0.0).astype(jnp.bfloat16)


def forward_body(
    len_ref, qkv_ref, cot_ref, own_ref, other_ref, prob_ref, token_ref, mix_ref, term_ref,
):
    rank = lax.axis_index("dp")
    first, second = clip_ends(len_ref, rank)

    def segment(shape, dim):
        place = lax.broadcasted_iota(jnp.int32, shape, dim)
        return (place >= first).astype(jnp.int32) + (place >= second).astype(jnp.int32)

    allowed = segment((TOK, TOK), 0) == segment((TOK, TOK), 1)
    for head in range(HEADS):
        start, stop = window(head)
        lanes = own_lanes(head)
        query = kept(lanes, qkv_ref[0, :, start:stop])
        value = kept(lanes, qkv_ref[2, :, start:stop])
        probs = attention(query, qkv_ref[1, :, start:stop], allowed).astype(jnp.bfloat16)
        prob_ref[head] = probs
        mixed = dot(probs, value, TN)
        offset = HSIZE * head - start
        if offset:
            mixed = pltpu.roll(mixed, stop - start - offset, 1)
        mix_ref[:, head * TILE:(head + 1) * TILE] = mixed[:, :TILE].astype(jnp.bfloat16)

    term_ref[...] = dot(cot_ref[...], mix_ref[...], TN)
    core = lax.rem(rank, NCORE)
    for z in range(NZ):
        for ref, part in ((own_ref, core), (other_ref, 1 - core)):
            rows = pl.ds(pl.multiple_of(2 * COLS * z + COLS * part, 8), COLS)
            for y in range(NY):
                ref[z * NY + y] = term_ref[rows, y * TILE:(y + 1) * TILE].astype(jnp.bfloat16)
    token_ref[...] = jnp.zeros(token_ref.shape, jnp.float32)


class Tiles:
    def __init__(self, ref, mask):
        self.ref = ref
        self.mask = mask
        self.held = [[None] * (FEAT // TILE) for _ in range(3)]

    def add(self, which, head, part):
        start, stop = window(head)
        for tile in range(start // TILE, stop // TILE):
            piece = part[:, tile * TILE - start:(tile + 1) * TILE - start]
            held = self.held[which][tile]
            held = piece if held is None else held + piece
            self.held[which][tile] = held
            if HSIZE * (head + 1) >= TILE * (tile + 1):
                if self.mask is not None:
                    held = jnp.where(self.mask, held, 0.0)
                self.ref[which, :, tile * TILE:(tile + 1) * TILE] = held.astype(jnp.bfloat16)


def add_gradient(tiles, head, rows_ref, probs, back):
    start, stop = window(head)
    lanes = own_lanes(head)
    query = kept(lanes, rows_ref[0, :, start:stop])
    key = kept(lanes, rows_ref[1, :, start:stop])
    grad_p = dot(rows_ref[2, :, start:stop], back, NT)
    wide = probs.astype(jnp.float32)
    weighted = wide * grad_p
    grad_s = weighted - wide * jnp.sum(weighted, axis=0, keepdims=True)
    grad_s = (grad_s * SCALE).astype(jnp.bfloat16)
    tiles.add(0, head, dot(grad_s, key, TN))
    tiles.add(1, head, dot(grad_s, query, NN))
    tiles.add(2, head, dot(probs, back, NN))


def fill_swap(swap_ref):
    lane = lax.broadcasted_iota(jnp.int32, (1, FEAT), 1)
    outer = lax.div(lane, HSIZE)
    inner = lax.div(lane - HSIZE * outer, ROWS)
    wanted = lane + (HSIZE - ROWS) * (inner - outer)
    for part in range(FEAT // HSIZE):
        rows = lax.broadcasted_iota(jnp.int32, (HSIZE, FEAT), 0) + HSIZE * part
        swap_ref[HSIZE * part:HSIZE * (part + 1), :] = as_bf16(rows == wanted)


def all_gradients(tiles, rows_ref, cot, prob_ref, weight_ref, swap_ref, back_ref):
    fill_swap(swap_ref)
    packed = dot(cot, weight_ref[...], NT).astype(jnp.bfloat16)
    back_ref[...] = dot(packed, swap_ref[...], NN).astype(jnp.bfloat16)
    for head in range(HEADS):
        start, stop = window(head)
        back = kept(own_lanes(head), back_ref[:, start:stop])
        add_gradient(tiles, head, rows_ref, prob_ref[head], back)


def box_backward_body(box_ref, prob_ref, weight_ref, send_ref, token_ref, swap_ref, back_ref):
    tiles = Tiles(send_ref, None)
    all_gradients(tiles, box_ref, box_ref[3], prob_ref, weight_ref, swap_ref, back_ref)
    token_ref[...] = jnp.zeros(token_ref.shape, jnp.float32)


def home_backward_body(
    len_ref, move_ref, qkv_ref, cot_ref, prob_ref, weight_ref, order_ref,
    home_ref, token_ref, swap_ref, back_ref,
):
    rank = lax.axis_index("dp")
    begin, count = moved_clip(len_ref, move_ref, rank)
    place = lax.broadcasted_iota(jnp.int32, (TOK, TILE), 0)
    tiles = Tiles(home_ref, (place < begin) | (place >= begin + count))
    all_gradients(tiles, qkv_ref, cot_ref[...], prob_ref, weight_ref, swap_ref, back_ref)
    token_ref[...] = order_ref[...]


def compact_body(column_ref, shard_ref, wide_ref):
    for y in range(NY):
        wide_ref[ROWS * y:ROWS * (y + 1), :] = column_ref[y].astype(jnp.float32)[:ROWS]
    shard_ref[...] = wide_ref[...].astype(jnp.bfloat16)


def copies_body(shard_ref, copies_ref):
    shard = shard_ref[...].astype(jnp.float32)
    shard = jnp.concatenate([shard, jnp.zeros((16 - ROWS, FEAT), jnp.float32)], axis=0)
    shard = shard.astype(jnp.bfloat16)
    for y in range(NY):
        copies_ref[y] = shard


def plane_body(got_ref, out_ref, turned_ref):
    total = jnp.sum(got_ref[...].astype(jnp.float32), axis=0)
    total = jnp.concatenate([total, jnp.zeros((TILE - COLS, TILE), jnp.float32)], axis=0)
    turned_ref[...] = jnp.transpose(total)
    out_ref[...] = jnp.zeros(out_ref.shape, jnp.float32)
    for x in range(NX):
        for b in range(2):
            rows = turned_ref[pl.ds(ROWS * x + b, ROWS // 2, stride=2), :]
            out_ref[x, :ROWS // 2, b * COLS:(b + 1) * COLS] = rows[:, :COLS]


def row_body(got_ref, order_ref, out_ref):
    total = jnp.sum(got_ref[...], axis=0)
    for b in range(2):
        out_ref[pl.ds(b, ROWS // 2, stride=2), :] = total[:ROWS // 2, b * COLS:(b + 1) * COLS]


def in_vmem():
    return pl.BlockSpec(memory_space=pltpu.VMEM)


def in_smem():
    return pl.BlockSpec(memory_space=pltpu.SMEM)


def shape_of(shape, dtype):
    return jax.ShapeDtypeStruct(shape, dtype)


TOKEN = shape_of((8, TILE), jnp.float32)


def kernel(body, name, outs, scalars, arrays, scratch=(), flops=100_000_000):
    return pl.pallas_call(
        body,
        out_shape=outs,
        in_specs=[in_smem()] * len(scalars) + [in_vmem()] * len(arrays),
        out_specs=tuple(in_vmem() for _ in outs),
        scratch_shapes=list(scratch),
        compiler_params=pltpu.CompilerParams(vmem_limit_bytes=VMEM_BYTES),
        cost_estimate=pl.CostEstimate(flops=flops, bytes_accessed=4_000_000, transcendentals=0),
        name=name,
    )(*scalars, *arrays)


def after(value, *others):
    return lax.optimization_barrier((value,) + others)[0]


def local(qkv, grad_out, lengths, moves, out_weight):
    rows = jnp.transpose(qkv[0, 0], (1, 0, 2))
    cot = grad_out[0, 0]
    counts = jnp.transpose(lengths, (2, 1, 0))
    moving = moves[0]
    ranks = NZ * NCORE
    bf16 = jnp.bfloat16

    with jax.named_scope("weights_y"):
        (copies,) = kernel(
            copies_body, "copies", (shape_of((NY, 16, FEAT), bf16),), (), (out_weight,)
        )
        column = lax.all_to_all(copies, "fsdp", 0, 0, tiled=True, axis_index_groups=Y_GROUPS)

    own, other, probs, token = kernel(
        forward_body,
        "forward",
        (
            shape_of((NZ * NY, COLS, TILE), bf16),
            shape_of((NZ * NY, COLS, TILE), bf16),
            shape_of((HEADS, TOK, TOK), bf16),
            TOKEN,
        ),
        (counts,),
        (rows, cot),
        scratch=(
            pltpu.VMEM((TOK, HEADS * TILE), bf16),
            pltpu.VMEM((FEAT, HEADS * TILE), jnp.float32),
        ),
        flops=3_000_000_000,
    )
    (column,) = kernel(
        compact_body, "compact", (shape_of((NY * ROWS, FEAT), bf16),), (),
        (after(column, token),), scratch=(pltpu.VMEM((NY * ROWS, FEAT), jnp.float32),),
    )
    with jax.named_scope("weights_x"):
        weights = lax.all_gather(
            column, "fsdp", axis=0, tiled=True, axis_index_groups=X_GROUPS
        )
    swapped = lax.ppermute(other, "dp", [(i, i + 1 - 2 * (i % NCORE)) for i in range(ranks)])
    pair = (own.astype(jnp.float32) + swapped.astype(jnp.float32)).astype(bf16)
    with jax.named_scope("reduce_zy"):
        got = lax.all_to_all(
            pair, ("dp", "fsdp"), 0, 0, tiled=True, axis_index_groups=PLANE_GROUPS
        )

    later = after(counts, token)
    (box,) = kernel(
        pack_body, "pack", (shape_of((4, CLIP_MAX, FEAT), bf16),), (later, moving), (rows, cot)
    )
    (box_probs,) = kernel(
        box_body, "box_forward", (shape_of((HEADS, CLIP_MAX, CLIP_MAX), bf16),),
        (later, moving), (box,), flops=1_000_000_000,
    )

    (plane,) = kernel(
        plane_body, "plane_sum", (shape_of((NX, 8, TILE), jnp.float32),), (), (got,),
        scratch=(pltpu.VMEM((TILE, TILE), jnp.float32),),
    )
    with jax.named_scope("reduce_x"):
        parts = lax.all_to_all(plane, "fsdp", 0, 0, tiled=True, axis_index_groups=X_GROUPS)
    weights = after(weights, plane)
    send, token = kernel(
        box_backward_body, "box_backward", (shape_of((3, CLIP_MAX, FEAT), bf16), TOKEN), (),
        (box, box_probs, weights),
        scratch=(pltpu.VMEM((FEAT, FEAT), bf16), pltpu.VMEM((CLIP_MAX, FEAT), bf16)), flops=3000000000,
    )
    inbox = lax.ppermute(send, "dp", [(i, (i + 1) % ranks) for i in range(ranks)])
    home, token = kernel(
        home_backward_body, "home_backward", (shape_of((3, TOK, FEAT), bf16), TOKEN),
        (counts, moving), (rows, cot, probs, weights, token),
        scratch=(pltpu.VMEM((FEAT, FEAT), bf16), pltpu.VMEM((TOK, FEAT), bf16)), flops=12000000000,
    )
    (weight_grad,) = kernel(
        row_body, "row_sum", (shape_of((ROWS, COLS), jnp.float32),), (), (parts, token)
    )
    return (
        jnp.transpose(home, (1, 0, 2))[None, None],
        jnp.transpose(inbox, (1, 0, 2))[None, None],
        weight_grad,
    )


def solution(mesh):
    placed = (
        P("dp", "fsdp", None, None, None),
        P("dp", "fsdp", None, None),
        P(None, "fsdp", None),
        P("fsdp", None, None),
        P("fsdp", None),
    )
    return jax.shard_map(
        local,
        mesh=mesh,
        in_specs=placed,
        out_specs=(
            P("dp", "fsdp", None, None, None),
            P("dp", "fsdp", None, None, None),
            P("fsdp", "dp"),
        ),
        check_vma=False,
    )
```

```python
import jax
import jax.numpy as jnp
import numpy as np
from jax import lax
from jax.experimental import pallas as pl
from jax.experimental.pallas import tpu as pltpu
from jax.sharding import PartitionSpec as P

HEADS = 8
HSIZE = 112
TOK = 192
CLIP_MAX = 128
FEAT = 896
NZ, NCORE, NY, NX = 8, 2, 8, 8
ROWS = 14
COLS = 56
SCALE = HSIZE ** (-0.5)
TILE = 128
VMEM_BYTES = 14 * 1024 * 1024

Y_GROUPS = [[y * NX + x for y in range(NY)] for x in range(NX)]
X_GROUPS = [[y * NX + x for x in range(NX)] for y in range(NY)]
PLANE_GROUPS = [
    [(z * NCORE + c) * NY * NX + y * NX + x for z in range(NZ) for y in range(NY)]
    for c in range(NCORE)
    for x in range(NX)
]
NT = (((1,), (1,)), ((), ()))
NN = (((1,), (0,)), ((), ()))
TN = (((0,), (0,)), ((), ()))


def dot(a, b, dims):
    return lax.dot_general(a, b, dims, preferred_element_type=jnp.float32)


def window(head):
    low = HSIZE * head
    start = TILE * (low // TILE)
    stop = TILE * (-(-(low + HSIZE) // TILE))
    return start, stop


def own_lanes(head):
    start, stop = window(head)
    lane = lax.broadcasted_iota(jnp.int32, (1, stop - start), 1) + start
    return (lane >= HSIZE * head) & (lane < HSIZE * (head + 1))


def kept(mask, value):
    return jnp.where(mask, value, jnp.zeros((), value.dtype))


def as_bf16(mask):
    return mask.astype(jnp.float32).astype(jnp.bfloat16)


def clip_ends(len_ref, rank):
    first = len_ref[0, 0, rank]
    return first, first + len_ref[1, 0, rank]


def moved_clip(len_ref, move_ref, source):
    first, second = clip_ends(len_ref, source)
    begin = jnp.int32(0)
    count = jnp.int32(0)
    for step in range(move_ref.shape[0]):
        mine = move_ref[step, 0] == source
        clip = move_ref[step, 2]
        clip_begin = jnp.where(clip == 0, 0, jnp.where(clip == 1, first, second))
        clip_end = jnp.where(clip == 0, first, jnp.where(clip == 1, second, TOK))
        begin = jnp.where(mine, clip_begin, begin)
        count = jnp.where(mine, clip_end - clip_begin, count)
    return begin, count


def attention(query, key, allowed):
    scores = dot(key, query, NT) * SCALE
    scores = jnp.where(allowed, scores, -1000000000.0)
    peak = jnp.max(scores, axis=0, keepdims=True)
    grown = jnp.exp(scores - peak)
    return grown * (1.0 / jnp.sum(grown, axis=0, keepdims=True))


def pack_body(len_ref, move_ref, qkv_ref, cot_ref, box_ref):
    rank = lax.axis_index("dp")
    begin, count = moved_clip(len_ref, move_ref, rank)
    row = lax.broadcasted_iota(jnp.int32, (CLIP_MAX, TOK), 0)
    col = lax.broadcasted_iota(jnp.int32, (CLIP_MAX, TOK), 1)
    pick = as_bf16((col == row + begin) & (row < count))
    for which in range(3):
        box_ref[which] = dot(pick, qkv_ref[which], NN).astype(jnp.bfloat16)
    box_ref[3] = dot(pick, cot_ref[...], NN).astype(jnp.bfloat16)


def box_body(len_ref, move_ref, box_ref, prob_ref):
    rank = lax.axis_index("dp")
    _, count = moved_clip(len_ref, move_ref, rank)
    row = lax.broadcasted_iota(jnp.int32, (CLIP_MAX, CLIP_MAX), 0)
    col = lax.broadcasted_iota(jnp.int32, (CLIP_MAX, CLIP_MAX), 1)
    for head in range(HEADS):
        start, stop = window(head)
        query = kept(own_lanes(head), box_ref[0, :, start:stop])
        probs = attention(query, box_ref[1, :, start:stop], row < count)
        prob_ref[head] = jnp.where(col < count, probs, 0.0).astype(jnp.bfloat16)


def forward_body(
    len_ref, qkv_ref, cot_ref, own_ref, other_ref, prob_ref, token_ref, mix_ref, term_ref,
):
    rank = lax.axis_index("dp")
    first, second = clip_ends(len_ref, rank)

    def segment(shape, dim):
        place = lax.broadcasted_iota(jnp.int32, shape, dim)
        return (place >= first).astype(jnp.int32) + (place >= second).astype(jnp.int32)

    allowed = segment((TOK, TOK), 0) == segment((TOK, TOK), 1)
    for head in range(HEADS):
        start, stop = window(head)
        lanes = own_lanes(head)
        query = kept(lanes, qkv_ref[0, :, start:stop])
        value = kept(lanes, qkv_ref[2, :, start:stop])
        probs = attention(query, qkv_ref[1, :, start:stop], allowed).astype(jnp.bfloat16)
        prob_ref[head] = probs
        mixed = dot(probs, value, TN)
        offset = HSIZE * head - start
        if offset:
            mixed = pltpu.roll(mixed, stop - start - offset, 1)
        mix_ref[:, head * TILE:(head + 1) * TILE] = mixed[:, :TILE].astype(jnp.bfloat16)

    term_ref[...] = dot(cot_ref[...], mix_ref[...], TN)
    core = lax.rem(rank, NCORE)
    for z in range(NZ):
        for ref, part in ((own_ref, core), (other_ref, 1 - core)):
            rows = pl.ds(pl.multiple_of(2 * COLS * z + COLS * part, 8), COLS)
            for y in range(NY):
                ref[z * NY + y] = term_ref[rows, y * TILE:(y + 1) * TILE].astype(jnp.bfloat16)
    token_ref[...] = jnp.zeros(token_ref.shape, jnp.float32)


class Tiles:
    def __init__(self, ref, mask):
        self.ref = ref
        self.mask = mask
        self.held = [[None] * (FEAT // TILE) for _ in range(3)]

    def add(self, which, head, part):
        start, stop = window(head)
        for tile in range(start // TILE, stop // TILE):
            piece = part[:, tile * TILE - start:(tile + 1) * TILE - start]
            held = self.held[which][tile]
            held = piece if held is None else held + piece
            self.held[which][tile] = held
            if HSIZE * (head + 1) >= TILE * (tile + 1):
                if self.mask is not None:
                    held = jnp.where(self.mask, held, 0.0)
                self.ref[which, :, tile * TILE:(tile + 1) * TILE] = held.astype(jnp.bfloat16)


def add_gradient(tiles, head, rows_ref, probs, back):
    start, stop = window(head)
    lanes = own_lanes(head)
    query = kept(lanes, rows_ref[0, :, start:stop])
    key = kept(lanes, rows_ref[1, :, start:stop])
    grad_p = dot(rows_ref[2, :, start:stop], back, NT)
    wide = probs.astype(jnp.float32)
    weighted = wide * grad_p
    grad_s = weighted - wide * jnp.sum(weighted, axis=0, keepdims=True)
    grad_s = (grad_s * SCALE).astype(jnp.bfloat16)
    tiles.add(0, head, dot(grad_s, key, TN))
    tiles.add(1, head, dot(grad_s, query, NN))
    tiles.add(2, head, dot(probs, back, NN))


def fill_swap(swap_ref):
    lane = lax.broadcasted_iota(jnp.int32, (1, FEAT), 1)
    outer = lax.div(lane, HSIZE)
    inner = lax.div(lane - HSIZE * outer, ROWS)
    wanted = lane + (HSIZE - ROWS) * (inner - outer)
    for part in range(FEAT // HSIZE):
        rows = lax.broadcasted_iota(jnp.int32, (HSIZE, FEAT), 0) + HSIZE * part
        swap_ref[HSIZE * part:HSIZE * (part + 1), :] = as_bf16(rows == wanted)


def all_gradients(tiles, rows_ref, cot, prob_ref, weight_ref, swap_ref, back_ref):
    fill_swap(swap_ref)
    packed = dot(cot, weight_ref[...], NT).astype(jnp.bfloat16)
    back_ref[...] = dot(packed, swap_ref[...], NN).astype(jnp.bfloat16)
    for head in range(HEADS):
        start, stop = window(head)
        back = kept(own_lanes(head), back_ref[:, start:stop])
        add_gradient(tiles, head, rows_ref, prob_ref[head], back)


def box_backward_body(box_ref, prob_ref, weight_ref, send_ref, token_ref, swap_ref, back_ref):
    tiles = Tiles(send_ref, None)
    all_gradients(tiles, box_ref, box_ref[3], prob_ref, weight_ref, swap_ref, back_ref)
    token_ref[...] = jnp.zeros(token_ref.shape, jnp.float32)


def home_backward_body(
    len_ref, move_ref, qkv_ref, cot_ref, prob_ref, weight_ref, order_ref,
    home_ref, token_ref, swap_ref, back_ref,
):
    rank = lax.axis_index("dp")
    begin, count = moved_clip(len_ref, move_ref, rank)
    place = lax.broadcasted_iota(jnp.int32, (TOK, TILE), 0)
    tiles = Tiles(home_ref, (place < begin) | (place >= begin + count))
    all_gradients(tiles, qkv_ref, cot_ref[...], prob_ref, weight_ref, swap_ref, back_ref)
    token_ref[...] = order_ref[...]


def compact_body(column_ref, shard_ref, wide_ref):
    for y in range(NY):
        wide_ref[ROWS * y:ROWS * (y + 1), :] = column_ref[y].astype(jnp.float32)
    shard_ref[...] = wide_ref[...].astype(jnp.bfloat16)


def plane_body(got_ref, out_ref, turned_ref):
    total = jnp.sum(got_ref[...].astype(jnp.float32), axis=0)
    total = jnp.concatenate([total, jnp.zeros((TILE - COLS, TILE), jnp.float32)], axis=0)
    turned_ref[...] = jnp.transpose(total)
    out_ref[...] = jnp.zeros(out_ref.shape, jnp.float32)
    for x in range(NX):
        for b in range(2):
            rows = turned_ref[pl.ds(ROWS * x + b, ROWS // 2, stride=2), :]
            out_ref[x, :ROWS // 2, b * COLS:(b + 1) * COLS] = rows[:, :COLS]


def row_body(got_ref, order_ref, out_ref):
    total = jnp.sum(got_ref[...], axis=0)
    for b in range(2):
        out_ref[pl.ds(b, ROWS // 2, stride=2), :] = total[:ROWS // 2, b * COLS:(b + 1) * COLS]


def in_vmem():
    return pl.BlockSpec(memory_space=pltpu.VMEM)


def in_smem():
    return pl.BlockSpec(memory_space=pltpu.SMEM)


def shape_of(shape, dtype):
    return jax.ShapeDtypeStruct(shape, dtype)


TOKEN = shape_of((8, TILE), jnp.float32)


def kernel(body, name, outs, scalars, arrays, scratch=(), flops=100_000_000):
    return pl.pallas_call(
        body,
        out_shape=outs,
        in_specs=[in_smem()] * len(scalars) + [in_vmem()] * len(arrays),
        out_specs=tuple(in_vmem() for _ in outs),
        scratch_shapes=list(scratch),
        compiler_params=pltpu.CompilerParams(vmem_limit_bytes=VMEM_BYTES),
        cost_estimate=pl.CostEstimate(flops=flops, bytes_accessed=4_000_000, transcendentals=0),
        name=name,
    )(*scalars, *arrays)


def after(value, *others):
    return lax.optimization_barrier((value,) + others)[0]


def local(qkv, grad_out, lengths, moves, out_weight):
    rows = jnp.transpose(qkv[0, 0], (1, 0, 2))
    cot = grad_out[0, 0]
    counts = jnp.transpose(lengths, (2, 1, 0))
    moving = moves[0]
    ranks = NZ * NCORE
    bf16 = jnp.bfloat16

    with jax.named_scope("weights_y"):
        copies = jnp.broadcast_to(out_weight[None], (NY,) + out_weight.shape)
        column = lax.all_to_all(copies, "fsdp", 0, 0, tiled=True, axis_index_groups=Y_GROUPS)

    own, other, probs, token = kernel(
        forward_body,
        "forward",
        (
            shape_of((NZ * NY, COLS, TILE), bf16),
            shape_of((NZ * NY, COLS, TILE), bf16),
            shape_of((HEADS, TOK, TOK), bf16),
            TOKEN,
        ),
        (counts,),
        (rows, cot),
        scratch=(
            pltpu.VMEM((TOK, HEADS * TILE), bf16),
            pltpu.VMEM((FEAT, HEADS * TILE), jnp.float32),
        ),
        flops=3_000_000_000,
    )
    (column,) = kernel(
        compact_body, "compact", (shape_of((NY * ROWS, FEAT), bf16),), (),
        (after(column, token),), scratch=(pltpu.VMEM((NY * ROWS, FEAT), jnp.float32),),
    )
    with jax.named_scope("weights_x"):
        weights = lax.all_gather(
            column, "fsdp", axis=0, tiled=True, axis_index_groups=X_GROUPS
        )
    swapped = lax.ppermute(other, "dp", [(i, i + 1 - 2 * (i % NCORE)) for i in range(ranks)])
    pair = (own.astype(jnp.float32) + swapped.astype(jnp.float32)).astype(bf16)
    with jax.named_scope("reduce_zy"):
        got = lax.all_to_all(
            pair, ("dp", "fsdp"), 0, 0, tiled=True, axis_index_groups=PLANE_GROUPS
        )

    later = after(counts, token)
    (box,) = kernel(
        pack_body, "pack", (shape_of((4, CLIP_MAX, FEAT), bf16),), (later, moving), (rows, cot)
    )
    (box_probs,) = kernel(
        box_body, "box_forward", (shape_of((HEADS, CLIP_MAX, CLIP_MAX), bf16),),
        (later, moving), (box,), flops=1_000_000_000,
    )

    (plane,) = kernel(
        plane_body, "plane_sum", (shape_of((NX, 8, TILE), jnp.float32),), (), (got,),
        scratch=(pltpu.VMEM((TILE, TILE), jnp.float32),),
    )
    with jax.named_scope("reduce_x"):
        parts = lax.all_to_all(plane, "fsdp", 0, 0, tiled=True, axis_index_groups=X_GROUPS)
    weights = after(weights, plane)
    send, token = kernel(
        box_backward_body, "box_backward", (shape_of((3, CLIP_MAX, FEAT), bf16), TOKEN), (),
        (box, box_probs, weights),
        scratch=(pltpu.VMEM((FEAT, FEAT), bf16), pltpu.VMEM((CLIP_MAX, FEAT), bf16)), flops=3000000000,
    )
    inbox = lax.ppermute(send, "dp", [(i, (i + 1) % ranks) for i in range(ranks)])
    home, token = kernel(
        home_backward_body, "home_backward", (shape_of((3, TOK, FEAT), bf16), TOKEN),
        (counts, moving), (rows, cot, probs, weights, token),
        scratch=(pltpu.VMEM((FEAT, FEAT), bf16), pltpu.VMEM((TOK, FEAT), bf16)), flops=12000000000,
    )
    (weight_grad,) = kernel(
        row_body, "row_sum", (shape_of((ROWS, COLS), jnp.float32),), (), (parts, token)
    )
    return (
        jnp.transpose(home, (1, 0, 2))[None, None],
        jnp.transpose(inbox, (1, 0, 2))[None, None],
        weight_grad,
    )


def solution(mesh):
    placed = (
        P("dp", "fsdp", None, None, None),
        P("dp", "fsdp", None, None),
        P(None, "fsdp", None),
        P("fsdp", None, None),
        P("fsdp", None),
    )
    return jax.shard_map(
        local,
        mesh=mesh,
        in_specs=placed,
        out_specs=(
            P("dp", "fsdp", None, None, None),
            P("dp", "fsdp", None, None, None),
            P("fsdp", "dp"),
        ),
        check_vma=False,
    )
```
